512 devices in a mesh: own: 128 (over y, z, core), rep: 4 (over x).
Axes of the slice: x: 4, y: 8, z: 8, core: 2. Of those that a mesh axis runs over, the one named last changes fastest.
Arguments:
- node_rows: bfloat16 [65536, 256], P(('own', 'rep')), may hold values from -6 to 6
- w_query: bfloat16 [256, 256], replicated, may hold values from -0.375 to 0.375
- w_keyval: bfloat16 [256, 512], replicated, may hold values from -0.375 to 0.375
- need_rows: int32 [128, 128, 4, 1], P(None, 'own'), may hold values from 0 to 127
- neighbours: int32 [65536, 16], P(('own', 'rep')), may hold values from 0 to 1023, as said below
- grad_out: bfloat16 [65536, 256], P(('own', 'rep')), may hold values from -6 to 6
Outputs:
- attended: bfloat16 [65536, 256], P(('own', 'rep'))
- grad_nodes: bfloat16 [65536, 256], P(('own', 'rep'))
- grad_query: float32 [256, 256], replicated
- grad_keyval: float32 [256, 512], replicated
The draws below stay inside these ranges and needn't reach their ends.
Inputs may be any that keep to these rules, and one draw needn't show every extreme that they name: `neighbours`: the first 2 entries of each node's list together name every received row of its group's table; the rest are spread over the whole table.
All inputs are finite; a program needn't handle non-finite values.
Results may differ from the reference program's by a relative error of at most 0.02.
Values may be sent and summed in bfloat16 or wider, within the bound.
No kernel may reach another device: no remote copies, remote signals or barrier semaphores. Data moves between devices by JAX's collectives and lax.ppermute only.
A program may use at most 64 MiB of HBM per device.

```python
import math
import jax
import jax.numpy as jnp
from jax import lax

HEADS = 4
HEAD_DIM = 64
D = 256
ROWS = 128
CAP = 1
DEG = 16
NODES = 65536
N_OWN = 128
N_REP = 4


def draw_neighbours(key, part):
    key = jax.random.fold_in(key, 7)
    group_size = N_REP * ROWS
    received = N_REP * N_OWN * CAP
    table_size = group_size + received
    order_keys = jax.random.split(jax.random.fold_in(key, 1), N_OWN)
    orders = jax.vmap(lambda single: jax.random.permutation(single, received))(order_keys)
    position = (jnp.arange(group_size, dtype=jnp.int32)[:, None] * 2 + jnp.arange(2, dtype=jnp.int32)[None, :]) % received
    covered = orders[:, position].astype(jnp.int32) + group_size
    others = jax.random.randint(jax.random.fold_in(key, 2), (N_OWN, group_size, DEG - 2), 0, table_size, dtype=jnp.int32)
    return jnp.concatenate([covered, others], 2).reshape(N_OWN * group_size, DEG).astype(jnp.int32)


def place_ends(entries, stream_key, least, high):
    longest = entries.shape.index(max(entries.shape))
    spots = []
    for shift in (0, 1):
        where = [jax.random.randint(jax.random.fold_in(stream_key, axis), (), 0, length) for axis, length in enumerate(entries.shape)]
        where[longest] = (where[longest] + shift) % entries.shape[longest]
        spots.append(tuple(where))
    return entries.at[spots[0]].set(least).at[spots[1]].set(high)


def block_scale(key, dims, cuts, least, largest):
    loudness, own = 1.0, jax.random.fold_in(key, 6)
    for dim, parts in cuts:
        steps = jnp.exp(jax.random.uniform(jax.random.fold_in(own, dim), (parts,), jnp.float32, least / len(cuts), largest / len(cuts)))
        loudness = loudness * jnp.repeat(steps, dims[dim] // parts).reshape([-1 if axis == dim else 1 for axis in range(len(dims))])
    return loudness


def centred(key, dims, scale, limit, cuts=(), kind=jnp.bfloat16):
    loudness = block_scale(key, dims, cuts, -0.22, 0.18) if cuts else 1.0
    result = jax.random.normal(key, dims, jnp.float32) * scale * loudness
    return jnp.minimum(jnp.maximum(result, -limit), limit).astype(kind)


def setup_inputs(seed: int = 0) -> dict:
    arg_keys = jax.random.split(jax.random.key(seed), 7)
    return {
        "node_rows": centred(arg_keys[0], (NODES, D), 1.0, 6.0, ((0, 512),)),
        "w_query": centred(arg_keys[1], (D, D), D ** -0.5, 0.375),
        "w_keyval": centred(arg_keys[2], (D, 2 * D), D ** -0.5, 0.375),
        "need_rows": place_ends(jax.random.randint(arg_keys[3], (N_OWN, N_OWN, N_REP, CAP), 0, ROWS), jax.random.fold_in(arg_keys[3], 1), 0, ROWS - 1).astype(jnp.int32),
        "neighbours": draw_neighbours(jax.random.fold_in(arg_keys[6], 71), 0),
        "grad_out": centred(arg_keys[5], (NODES, D), 1.0, 6.0, ((0, 512),)),
    }


HIGH = lax.Precision.HIGHEST

def rounded(value):
    return lax.optimization_barrier(value.astype(jnp.bfloat16)).astype(jnp.float32)

def reference(node_rows, w_query, w_keyval, need_rows, neighbours, grad_out):
    group_size = N_REP * ROWS
    received = N_REP * N_OWN * CAP
    table_size = group_size + received
    features = HEADS * HEAD_DIM
    score_scale = 1.0 / math.sqrt(HEAD_DIM)
    query_all = jnp.dot(node_rows, w_query, preferred_element_type=jnp.float32).astype(jnp.bfloat16)
    keyval_all = jnp.dot(node_rows, w_keyval, preferred_element_type=jnp.float32).astype(jnp.bfloat16)
    source = jnp.arange(N_OWN, dtype=jnp.int32)[None, :, None, None]
    replica = jnp.arange(N_REP, dtype=jnp.int32)[None, None, :, None]
    remote = (source * N_REP + replica) * ROWS + need_rows.astype(jnp.int32)
    remote = jnp.transpose(remote, (0, 2, 1, 3)).reshape(N_OWN, received)
    local_ids = jnp.arange(N_OWN, dtype=jnp.int32)[:, None] * group_size + jnp.arange(group_size, dtype=jnp.int32)[None, :]
    table_ids = jnp.concatenate([local_ids, remote], 1).astype(jnp.int32)
    links_all = neighbours.reshape(N_OWN, group_size, DEG).astype(jnp.int32)
    wq32 = w_query.astype(jnp.float32)
    wkv32 = w_keyval.astype(jnp.float32)
    device_of = (jnp.arange(group_size, dtype=jnp.int32) // ROWS)[:, None]

    def per_group(carry, inputs):
        grad_nodes, grad_q, grad_kv = carry
        ids, links, owner = inputs
        start = (owner * group_size).astype(jnp.int32)
        queries = lax.dynamic_slice_in_dim(query_all, start, group_size, 0).astype(jnp.float32).reshape(group_size, HEADS, HEAD_DIM)
        upstream = lax.dynamic_slice_in_dim(grad_out, start, group_size, 0).astype(jnp.float32).reshape(group_size, HEADS, HEAD_DIM)
        own_nodes = lax.dynamic_slice_in_dim(node_rows, start, group_size, 0).astype(jnp.float32)
        gathered = keyval_all[ids[links]].astype(jnp.float32)
        key_rows = gathered[:, :, :features].reshape(group_size, DEG, HEADS, HEAD_DIM)
        value_rows = gathered[:, :, features:].reshape(group_size, DEG, HEADS, HEAD_DIM)
        scores = jnp.einsum('ghd,gjhd->gjh', queries, key_rows, precision=HIGH) * score_scale
        weights = jnp.exp(scores)
        attention = weights / lax.optimization_barrier(jnp.sum(weights, axis=1, keepdims=True))
        attention_b = rounded(attention)
        attended = jnp.einsum('gjh,gjhd->ghd', attention_b, value_rows, precision=HIGH).astype(jnp.bfloat16).reshape(group_size, features)
        dprob = jnp.einsum('ghd,gjhd->gjh', upstream, value_rows, precision=HIGH)
        dscore = rounded(attention * (dprob - lax.optimization_barrier(jnp.sum(attention * dprob, axis=1, keepdims=True))) * score_scale)
        dquery = rounded(jnp.einsum('gjh,gjhd->ghd', dscore, key_rows, precision=HIGH)).reshape(group_size, features)
        contrib_key = (dscore[..., None] * queries[:, None]).reshape(group_size, DEG, features)
        contrib_value = (attention_b[..., None] * upstream[:, None]).reshape(group_size, DEG, features)
        contrib = jnp.concatenate([contrib_key, contrib_value], 2).reshape(group_size * DEG, 2 * features)
        segment = (links + device_of * table_size).reshape(-1)
        partial_kv = jax.ops.segment_sum(contrib, segment, num_segments=N_REP * table_size)
        partial_kv = rounded(partial_kv).reshape(N_REP, table_size, 2 * features)
        partial_x = rounded(jnp.einsum('rtk,dk->rtd', partial_kv, wkv32, precision=HIGH))
        table_grad = lax.optimization_barrier(jnp.sum(partial_x, axis=0))
        grad_nodes = grad_nodes.at[ids].add(table_grad)
        local_grad = jnp.dot(dquery, wq32.T, precision=HIGH)
        grad_nodes = grad_nodes.at[start + jnp.arange(group_size, dtype=jnp.int32)].add(local_grad)
        table_x = node_rows[ids].astype(jnp.float32)
        grad_kv = grad_kv + jnp.dot(table_x.T, lax.optimization_barrier(jnp.sum(partial_kv, axis=0)), precision=HIGH)
        grad_q = grad_q + jnp.dot(own_nodes.T, dquery, precision=HIGH)
        return ((grad_nodes, grad_q, grad_kv), attended)
    start_carry = (jnp.zeros((NODES, features), jnp.float32), jnp.zeros((features, features), jnp.float32), jnp.zeros((features, 2 * features), jnp.float32))
    owners = jnp.arange(N_OWN, dtype=jnp.int32)
    final, attended = lax.scan(per_group, start_carry, (table_ids, links_all, owners))
    grad_nodes, grad_q, grad_kv = final
    return (attended.reshape(NODES, features), grad_nodes.astype(jnp.bfloat16), grad_q, grad_kv)
```

```python
import math

import jax
import jax.numpy as jnp
from jax import lax
from jax.experimental import pallas as pl
from jax.experimental.pallas import tpu as pltpu
from jax.sharding import Mesh
from jax.sharding import PartitionSpec as P

HEADS = 4
HEAD_DIM = 64
LANES = 128
BF16, F32 = jnp.bfloat16, jnp.float32


def dot(a, b, contract=((1,), (0,))):
    return lax.dot_general(a, b, (contract, ((), ())), preferred_element_type=F32)


def rows_of_both(a, b):
    return dot(a, b, ((1,), (1,)))


def columns_of_both(a, b):
    return dot(a, b, ((0,), (0,)))


def exchange(blocks, axes):
    return lax.all_to_all(blocks, axes, split_axis=0, concat_axis=0, tiled=True)


def spread(block, axes, count):
    return exchange(jnp.broadcast_to(block[None], (count,) + block.shape), axes)


def per_head(rows):
    head = lax.broadcasted_iota(jnp.int32, rows.shape, 1) // HEAD_DIM
    wide = rows.astype(F32)
    return jnp.concatenate([jnp.where(head == h, wide, 0.0) for h in range(HEADS)], 0)


def own_blocks(table, nodes):
    blocks = [
        table[h * HEAD_DIM : (h + 1) * HEAD_DIM, h * nodes : (h + 1) * nodes] for h in range(HEADS)
    ]
    return jnp.concatenate(blocks, 0).T


def attention_kernel(
    node_ref, grad_ref, links_ref, table_ref, wq_ref, wkv_ref,
    attended_ref, send_ref, dnode_ref, weight_scr, dprob_scr,
):
    nodes, features = node_ref.shape
    degree = links_ref.shape[0]
    replicas = send_ref.shape[0]
    block = table_ref.shape[0] // replicas
    scale = 1.0 / math.sqrt(HEAD_DIM)
    node = node_ref[...]
    wkv = wkv_ref[...]
    queries = per_head(dot(node, wq_ref[...]).astype(BF16))
    upstream = per_head(grad_ref[...])
    q_heads, q_scaled = queries.astype(BF16), (queries * scale).astype(BF16)
    g_heads, g_scaled = upstream.astype(BF16), (upstream * scale).astype(BF16)

    links = links_ref[...]
    arrived = links >= replicas * nodes
    owner = jnp.where(arrived, links - replicas * nodes, links) // nodes
    links = owner * block + jnp.where(arrived, nodes, 0) + links % nodes

    keyval = []
    total = jnp.zeros((1, HEADS * nodes), F32)
    inner = jnp.zeros((1, HEADS * nodes), F32)
    for r in range(replicas):
        span = slice(r * block, (r + 1) * block)
        kv = dot(table_ref[span, :], wkv).astype(BF16)
        keyval.append(kv)
        here = lax.broadcasted_iota(jnp.int32, (block, nodes), 0) + r * block
        count = jnp.zeros((block, nodes), F32)
        for j in range(degree):
            count = count + jnp.where(here == links[j : j + 1, :], 1.0, 0.0)
        log_count = jnp.where(count > 0.0, jnp.log(jnp.maximum(count, 1.0)), -1e30)
        log_count = jnp.concatenate([log_count] * HEADS, 1)
        weight = jnp.exp(rows_of_both(kv[:, :features], q_scaled) + log_count)
        dprob = rows_of_both(kv[:, features:], g_scaled)
        total = total + jnp.sum(weight, axis=0, keepdims=True)
        inner = inner + jnp.sum(weight * dprob, axis=0, keepdims=True)
        weight_scr[span, :] = weight
        dprob_scr[span, :] = dprob

    inverse = 1.0 / total
    mean = inner * inverse
    attended = jnp.zeros((features, HEADS * nodes), F32)
    dquery = jnp.zeros((features, HEADS * nodes), F32)
    grad_kv = jnp.zeros(wkv.shape, F32)
    for r in range(replicas):
        span = slice(r * block, (r + 1) * block)
        kv = keyval[r]
        prob = weight_scr[span, :] * inverse
        dscore = (prob * (dprob_scr[span, :] - mean)).astype(BF16)
        prob = prob.astype(BF16)
        attended = attended + columns_of_both(kv[:, features:], prob)
        dquery = dquery + columns_of_both(kv[:, :features], dscore)
        dkv = jnp.concatenate([dot(dscore, q_heads), dot(prob, g_heads)], 1).astype(BF16)
        grad_kv = grad_kv + columns_of_both(table_ref[span, :], dkv)
        dsrc = rows_of_both(dkv, wkv).astype(BF16)
        for part in range(2):
            for half in range(2):
                at = (part * 2 + half) * nodes
                send_ref[r, at : at + nodes, :] = dsrc[
                    part * nodes : (part + 1) * nodes, half * LANES : (half + 1) * LANES
                ]

    attended_ref[...] = own_blocks(attended, nodes).astype(BF16)
    dquery = own_blocks(dquery, nodes).astype(BF16)
    dnode_ref[...] = rows_of_both(dquery, wq_ref[...])
    grads = jnp.concatenate([columns_of_both(node, dquery), grad_kv], 1).astype(BF16)
    pieces = features * grads.shape[1] // (LANES * LANES)
    each = pieces // replicas
    down = features // LANES
    for piece in range(pieces):
        column, row = (piece // down) * LANES, (piece % down) * LANES
        at = 4 * nodes + (piece % each) * LANES
        send_ref[piece // each, at : at + LANES, :] = grads[row : row + LANES, column : column + LANES]


def attention(node_rows, grad_out, links, table, w_query, w_keyval, replicas):
    nodes, features = node_rows.shape
    entries = table.shape[0]
    sent = 4 * nodes + features * (features + w_keyval.shape[1]) // LANES // replicas
    whole = pl.BlockSpec(memory_space=pltpu.VMEM)
    return pl.pallas_call(
        attention_kernel,
        out_shape=(
            jax.ShapeDtypeStruct((nodes, features), BF16),
            jax.ShapeDtypeStruct((replicas, sent, LANES), BF16),
            jax.ShapeDtypeStruct((nodes, features), F32),
        ),
        in_specs=[whole] * 6,
        out_specs=(whole,) * 3,
        scratch_shapes=[pltpu.VMEM((entries, HEADS * nodes), F32)] * 2,
        compiler_params=pltpu.CompilerParams(vmem_limit_bytes=48 * 1024 * 1024),
        name="attention",
    )(node_rows, grad_out, links, table, w_query, w_keyval)


def shards(node_rows, w_query, w_keyval, need_rows, neighbours, grad_out):
    nodes, features = node_rows.shape
    ny, nz, nc, replicas = (lax.axis_size(a) for a in ("y", "z", "c", "x"))
    inner = nz * nc
    owners = ny * inner

    wanted = need_rows.reshape(owners, replicas).T
    my_rows = lax.dynamic_index_in_dim(wanted, lax.axis_index("x"), 0, keepdims=False)
    picks = (my_rows[:, None] == jnp.arange(nodes, dtype=jnp.int32)[None, :]).astype(BF16)
    outgoing = dot(picks, node_rows).astype(BF16)
    incoming = exchange(outgoing, ("y", "z", "c"))
    table = spread(jnp.concatenate([node_rows, incoming], 0), "x", replicas)
    table = table.reshape(-1, features)

    attended, partial, dnode = attention(
        node_rows, grad_out, neighbours.T, table, w_query, w_keyval, replicas
    )

    summed = jnp.sum(exchange(partial, "x").astype(F32), 0)
    own = jnp.concatenate([summed[:nodes], summed[nodes : 2 * nodes]], 1)
    back = summed[2 * nodes : 4 * nodes].astype(BF16).reshape(2, ny, inner, LANES)
    grads = summed[4 * nodes :].astype(BF16).reshape(inner, -1, LANES)
    kept = grads.shape[1]
    back = back.transpose(2, 0, 1, 3).reshape(inner, 2 * ny, LANES)
    landed = exchange(jnp.concatenate([back, grads], 1), ("z", "c"))
    back = landed[:, : 2 * ny].reshape(inner, 2, ny, LANES).transpose(2, 1, 0, 3)
    back = back.reshape(ny, 2 * inner, LANES)
    grads = jnp.sum(landed[:, 2 * ny :].astype(F32), 0).astype(BF16)
    grads = jnp.broadcast_to(grads[None], (ny, kept, LANES))
    landed = exchange(jnp.concatenate([back, grads], 1), "y")
    returned = jnp.concatenate(
        [
            landed[:, :inner].reshape(owners, LANES),
            landed[:, inner : 2 * inner].reshape(owners, LANES),
        ],
        1,
    )
    grad_nodes = (own + dnode + columns_of_both(picks, returned)).astype(BF16)
    grads = jnp.sum(landed[:, 2 * inner :].astype(F32), 0).astype(BF16)
    grads = spread(grads, ("z", "c"), inner).reshape(-1, LANES)
    grads = spread(grads, "x", replicas).reshape(-1, features, LANES).astype(F32)
    grads = grads.transpose(1, 0, 2).reshape(features, -1)
    return attended, grad_nodes, grads[:, :features], grads[:, features:]


def solution(mesh):
    own, rep = mesh.devices.shape
    side = math.isqrt(own // 2)
    fine = Mesh(mesh.devices.reshape(side, own // 2 // side, 2, rep), ("y", "z", "c", "x"))
    rows = P(("y", "z", "c", "x"), None)
    in_specs = (rows, P(), P(), P(None, ("y", "z", "c"), None, None), rows, rows)
    return jax.shard_map(
        shards, mesh=fine, in_specs=in_specs, out_specs=(rows, rows, P(), P()), check_vma=False
    )
```

```python
import math

import jax
import jax.numpy as jnp
from jax import lax
from jax.experimental import pallas as pl
from jax.experimental.pallas import tpu as pltpu
from jax.sharding import Mesh
from jax.sharding import PartitionSpec as P

HEADS = 4
HEAD_DIM = 64
LANES = 128
SMALL = 8 * 1024 * 1024
BF16, F32 = jnp.bfloat16, jnp.float32


def dot(a, b, contract=((1,), (0,))):
    return lax.dot_general(a, b, (contract, ((), ())), preferred_element_type=F32)


def rows_of_both(a, b):
    return dot(a, b, ((1,), (1,)))


def columns_of_both(a, b):
    return dot(a, b, ((0,), (0,)))


def exchange(blocks, axes):
    return lax.all_to_all(blocks, axes, split_axis=0, concat_axis=0, tiled=True)


def spread(block, axes, count):
    return exchange(jnp.broadcast_to(block[None], (count,) + block.shape), axes)


def per_head(rows):
    head = lax.broadcasted_iota(jnp.int32, rows.shape, 1) // HEAD_DIM
    wide = rows.astype(F32)
    return jnp.concatenate([jnp.where(head == h, wide, 0.0) for h in range(HEADS)], 0)


def per_pair(values, weights):
    wide, long = weights.shape[1] // (HEADS // 2), 2 * HEAD_DIM
    pairs = [
        columns_of_both(values[:, p * long : (p + 1) * long], weights[:, p * wide : (p + 1) * wide])
        for p in range(HEADS // 2)
    ]
    return jnp.concatenate(pairs, 0)


def own_blocks(table, nodes):
    blocks = [
        table[h * HEAD_DIM : (h + 1) * HEAD_DIM, h % 2 * nodes : (h % 2 + 1) * nodes]
        for h in range(HEADS)
    ]
    return jnp.concatenate(blocks, 0).T


def pick_kernel(rows_ref, node_ref, out_ref, kept_ref):
    kept_ref[...] = node_ref[...]
    nodes = node_ref.shape[0]
    picks = lax.broadcasted_iota(jnp.int32, (nodes, rows_ref.shape[1]), 0) == rows_ref[...]
    picks = jnp.where(picks, 1.0, 0.0).astype(BF16)
    out_ref[...] = columns_of_both(picks, node_ref[...]).astype(BF16)


def finish_kernel(
    rows_ref, landed_ref, summed_ref, dnode_ref, grads_ref, attended_in_ref,
    attended_ref, nodes_ref, grad_q_ref, grad_kv_ref,
):
    nodes, features = dnode_ref.shape
    outer, _, lanes = landed_ref.shape
    owners = rows_ref.shape[1]
    inner = owners // outer
    attended_ref[...] = attended_in_ref[...]
    each = grads_ref.shape[1]
    down = features // LANES
    for piece in range(grads_ref.shape[0] * each // LANES):
        at = piece % (each // LANES) * LANES
        block = grads_ref[piece // (each // LANES), at : at + LANES, :].astype(F32)
        column, row = (piece // down) * LANES, (piece % down) * LANES
        if column < features:
            grad_q_ref[row : row + LANES, column : column + LANES] = block
        else:
            column = column - features
            grad_kv_ref[row : row + LANES, column : column + LANES] = block
    picks = lax.broadcasted_iota(jnp.int32, (nodes, owners), 0) == rows_ref[...]
    picks = jnp.where(picks, 1.0, 0.0).astype(BF16)
    for half in range(features // LANES):
        at = slice(half * LANES, (half + 1) * LANES)
        back = landed_ref[:, half * inner : (half + 1) * inner, :].reshape(owners, lanes)
        total = summed_ref[half * nodes : (half + 1) * nodes, :] + dnode_ref[:, at]
        nodes_ref[:, at] = (total + dot(picks, back)).astype(BF16)


def attention_kernel(
    node_ref, grad_ref, links_ref, table_ref, wq_ref, wkv_ref,
    attended_ref, send_ref, dnode_ref, weight_scr, dprob_scr,
):
    nodes, features = node_ref.shape
    degree = links_ref.shape[0]
    replicas = send_ref.shape[0]
    block = table_ref.shape[0] // replicas
    scale = 1.0 / math.sqrt(HEAD_DIM)
    node = node_ref[...]
    wkv = wkv_ref[...]
    queries = per_head(dot(node, wq_ref[...]).astype(BF16))
    upstream = per_head(grad_ref[...])
    q_heads, q_scaled = queries.astype(BF16), (queries * scale).astype(BF16)
    g_heads, g_scaled = upstream.astype(BF16), (upstream * scale).astype(BF16)

    links = links_ref[...]
    arrived = links >= replicas * nodes
    owner = jnp.where(arrived, links - replicas * nodes, links) // nodes
    links = owner * block + jnp.where(arrived, nodes, 0) + links % nodes

    keyval = []
    whole_kv = dot(table_ref[...], wkv).astype(BF16)
    total = jnp.zeros((1, HEADS * nodes), F32)
    inner = jnp.zeros((1, HEADS * nodes), F32)
    for r in range(replicas):
        span = slice(r * block, (r + 1) * block)
        kv = whole_kv[span, :]
        keyval.append(kv)
        here = (lax.broadcasted_iota(jnp.int32, (block, nodes), 0) + r * block).astype(jnp.int16)
        count = jnp.zeros((block, nodes), BF16)
        for j in range(degree):
            hit = here == jnp.broadcast_to(links[j : j + 1, :].astype(jnp.int16), here.shape)
            count = count + jnp.where(hit, jnp.ones_like(count), jnp.zeros_like(count))
        count = count.astype(F32)
        log_count = jnp.where(count > 0.0, jnp.log(jnp.maximum(count, 1.0)), -1e30)
        log_count = jnp.concatenate([log_count] * HEADS, 1)
        weight = jnp.exp(rows_of_both(kv[:, :features], q_scaled) + log_count)
        dprob = rows_of_both(kv[:, features:], g_scaled)
        total = total + jnp.sum(weight, axis=0, keepdims=True)
        inner = inner + jnp.sum(weight * dprob, axis=0, keepdims=True)
        weight_scr[span, :] = weight
        dprob_scr[span, :] = dprob

    inverse = 1.0 / total
    mean = inner * inverse
    attended = jnp.zeros((features, 2 * nodes), F32)
    dquery = jnp.zeros((features, 2 * nodes), F32)
    all_dkv = []
    for r in range(replicas):
        span = slice(r * block, (r + 1) * block)
        kv = keyval[r]
        prob = weight_scr[span, :] * inverse
        dscore = (prob * (dprob_scr[span, :] - mean)).astype(BF16)
        prob = prob.astype(BF16)
        attended = attended + per_pair(kv[:, features:], prob)
        dquery = dquery + per_pair(kv[:, :features], dscore)
        dkv = jnp.concatenate([dot(dscore, q_heads), dot(prob, g_heads)], 1).astype(BF16)
        all_dkv.append(dkv)
        dsrc = rows_of_both(dkv, wkv).astype(BF16)
        for part in range(2):
            for half in range(2):
                at = (part * 2 + half) * nodes
                send_ref[r, at : at + nodes, :] = dsrc[
                    part * nodes : (part + 1) * nodes, half * LANES : (half + 1) * LANES
                ]

    grad_kv = columns_of_both(table_ref[...], jnp.concatenate(all_dkv, 0))
    attended_ref[...] = own_blocks(attended, nodes).astype(BF16)
    dquery = own_blocks(dquery, nodes).astype(BF16)
    dnode_ref[...] = rows_of_both(dquery, wq_ref[...])
    grads = jnp.concatenate([columns_of_both(node, dquery), grad_kv], 1).astype(BF16)
    pieces = features * grads.shape[1] // (LANES * LANES)
    each = pieces // replicas
    down = features // LANES
    for piece in range(pieces):
        column, row = (piece // down) * LANES, (piece % down) * LANES
        at = 4 * nodes + (piece % each) * LANES
        send_ref[piece // each, at : at + LANES, :] = grads[row : row + LANES, column : column + LANES]


def attention(node_rows, grad_out, links, table, w_query, w_keyval, replicas):
    nodes, features = node_rows.shape
    entries = table.shape[0]
    sent = 4 * nodes + features * (features + w_keyval.shape[1]) // LANES // replicas
    whole = pl.BlockSpec(memory_space=pltpu.VMEM)
    return pl.pallas_call(
        attention_kernel,
        out_shape=(
            jax.ShapeDtypeStruct((nodes, features), BF16),
            jax.ShapeDtypeStruct((replicas, sent, LANES), BF16),
            jax.ShapeDtypeStruct((nodes, features), F32),
        ),
        in_specs=[whole] * 6,
        out_specs=(whole,) * 3,
        scratch_shapes=[pltpu.VMEM((entries, HEADS * nodes), F32)] * 2,
        compiler_params=pltpu.CompilerParams(vmem_limit_bytes=48 * 1024 * 1024),
        name="attention",
    )(node_rows, grad_out, links, table, w_query, w_keyval)


def shards(node_rows, w_query, w_keyval, need_rows, neighbours, grad_out):
    nodes, features = node_rows.shape
    ny, nz, nc, replicas = (lax.axis_size(a) for a in ("y", "z", "c", "x"))
    inner = nz * nc
    owners = ny * inner

    wanted = need_rows.reshape(owners, replicas).T
    my_rows = lax.dynamic_index_in_dim(wanted, lax.axis_index("x"), 0, keepdims=False)
    my_rows = my_rows[None, :]
    whole = pl.BlockSpec(memory_space=pltpu.VMEM)
    outgoing, kept = pl.pallas_call(
        pick_kernel,
        out_shape=(
            jax.ShapeDtypeStruct((owners, features), BF16),
            jax.ShapeDtypeStruct((nodes, features), BF16),
        ),
        in_specs=[whole] * 2,
        out_specs=(whole,) * 2,
        compiler_params=pltpu.CompilerParams(vmem_limit_bytes=SMALL),
        name="pick",
    )(my_rows, node_rows)
    incoming = exchange(outgoing.reshape(owners, -1, LANES), ("y", "z", "c")).reshape(owners, features)
    table = spread(jnp.concatenate([kept, incoming], 0), "x", replicas)
    table = table.reshape(-1, features)

    attended, partial, dnode = attention(
        kept, grad_out, neighbours.T, table, w_query, w_keyval, replicas
    )

    summed = jnp.sum(exchange(partial, "x").astype(F32), 0)
    back = summed[2 * nodes : 4 * nodes].astype(BF16).reshape(2, ny, inner, LANES)
    grads = summed[4 * nodes :].astype(BF16).reshape(inner, -1, LANES)
    each = grads.shape[1]
    back = back.transpose(2, 0, 1, 3).reshape(inner, 2 * ny, LANES)
    landed = exchange(jnp.concatenate([back, grads], 1), ("z", "c"))
    back = landed[:, : 2 * ny].reshape(inner, 2, ny, LANES).transpose(2, 1, 0, 3)
    back = back.reshape(ny, 2 * inner, LANES)
    grads = jnp.sum(landed[:, 2 * ny :].astype(F32), 0).astype(BF16)
    grads = jnp.broadcast_to(grads[None], (ny, each, LANES))
    landed = exchange(jnp.concatenate([back, grads], 1), "y")
    grads = jnp.sum(landed[:, 2 * inner :].astype(F32), 0).astype(BF16)
    grads = spread(grads, ("z", "c"), inner).reshape(-1, LANES)
    grads = spread(grads, "x", replicas)
    return pl.pallas_call(
        finish_kernel,
        out_shape=(
            jax.ShapeDtypeStruct((nodes, features), BF16),
            jax.ShapeDtypeStruct((nodes, features), BF16),
            jax.ShapeDtypeStruct(w_query.shape, F32),
            jax.ShapeDtypeStruct(w_keyval.shape, F32),
        ),
        in_specs=[whole] * 6,
        out_specs=(whole,) * 4,
        compiler_params=pltpu.CompilerParams(vmem_limit_bytes=SMALL),
        name="finish",
    )(my_rows, landed, summed, dnode, grads, attended)


def solution(mesh):
    own, rep = mesh.devices.shape
    side = math.isqrt(own // 2)
    fine = Mesh(mesh.devices.reshape(side, own // 2 // side, 2, rep), ("y", "z", "c", "x"))
    rows = P(("y", "z", "c", "x"), None)
    in_specs = (rows, P(), P(), P(None, ("y", "z", "c"), None, None), rows, rows)
    return jax.shard_map(
        shards, mesh=fine, in_specs=in_specs, out_specs=(rows, rows, P(), P()), check_vma=False
    )
```

```python
import itertools
import math

import jax
import jax.numpy as jnp
from jax import lax
from jax.experimental import pallas as pl
from jax.experimental.pallas import tpu as pltpu
from jax.sharding import Mesh
from jax.sharding import PartitionSpec as P

HEADS = 4
HEAD_DIM = 64
LANES = 128
SMALL = 8 * 1024 * 1024
BF16, F32 = jnp.bfloat16, jnp.float32


def dot(a, b, contract=((1,), (0,))):
    return lax.dot_general(a, b, (contract, ((), ())), preferred_element_type=F32)


def rows_of_both(a, b):
    return dot(a, b, ((1,), (1,)))


def columns_of_both(a, b):
    return dot(a, b, ((0,), (0,)))


def exchange(blocks, axes):
    return lax.all_to_all(blocks, axes, split_axis=0, concat_axis=0, tiled=True)


def spread(block, axes, count):
    return exchange(jnp.broadcast_to(block[None], (count,) + block.shape), axes)


def per_head(rows):
    head = lax.broadcasted_iota(jnp.int32, rows.shape, 1) // HEAD_DIM
    wide = rows.astype(F32)
    return jnp.concatenate([jnp.where(head == h, wide, 0.0) for h in range(HEADS)], 0)


def per_pair(values, weights):
    wide, long = weights.shape[1] // (HEADS // 2), 2 * HEAD_DIM
    pairs = [
        columns_of_both(values[:, p * long : (p + 1) * long], weights[:, p * wide : (p + 1) * wide])
        for p in range(HEADS // 2)
    ]
    return jnp.concatenate(pairs, 0)


def own_blocks(table, nodes):
    blocks = [
        table[h * HEAD_DIM : (h + 1) * HEAD_DIM, h % 2 * nodes : (h % 2 + 1) * nodes]
        for h in range(HEADS)
    ]
    return jnp.concatenate(blocks, 0).T


def pick_kernel(rows_ref, node_ref, out_ref, kept_ref):
    kept_ref[...] = node_ref[...]
    nodes = node_ref.shape[0]
    picks = lax.broadcasted_iota(jnp.int32, (nodes, rows_ref.shape[1]), 0) == rows_ref[...]
    picks = jnp.where(picks, 1.0, 0.0).astype(BF16)
    out_ref[...] = columns_of_both(picks, node_ref[...]).astype(BF16)


def finish_kernel(
    core_ref, rows_ref, landed_ref, summed_ref, dnode_ref, mine_ref, other_ref, attended_in_ref,
    attended_ref, nodes_ref, grad_q_ref, grad_kv_ref,
):
    nodes, features = dnode_ref.shape
    outer, _, lanes = landed_ref.shape
    owners = rows_ref.shape[1]
    inner = owners // outer
    cores = 2
    attended_ref[...] = attended_in_ref[...]
    replicas, depth, each, _ = mine_ref.shape
    for x, z, c in itertools.product(range(replicas), range(depth), range(cores)):
        block = jnp.where(core_ref[0] == c, mine_ref[x, z], other_ref[x, z]).astype(F32)
        first = ((x * cores + c) * depth + z) * each
        for row in range(first, first + each, 8):
            column, at = row // features * LANES, row % features
            to_ref = grad_q_ref if column < features else grad_kv_ref
            column = column if column < features else column - features
            to_ref[at : at + 8, column : column + LANES] = block[row - first : row - first + 8]
    picks = lax.broadcasted_iota(jnp.int32, (nodes, owners), 0) == rows_ref[...]
    picks = jnp.where(picks, 1.0, 0.0).astype(BF16)
    given = lax.broadcasted_iota(jnp.int32, (owners, owners), 0)
    asked = lax.broadcasted_iota(jnp.int32, (owners, owners), 1)
    asked = asked // inner * inner + asked % depth * cores + asked // depth % cores
    picks = dot(picks, jnp.where(given == asked, 1.0, 0.0).astype(BF16)).astype(BF16)
    for half in range(features // LANES):
        at = slice(half * LANES, (half + 1) * LANES)
        back = landed_ref[:, half * inner : (half + 1) * inner, :].reshape(owners, lanes)
        total = summed_ref[half * nodes : (half + 1) * nodes, :] + dnode_ref[:, at]
        nodes_ref[:, at] = (total + dot(picks, back)).astype(BF16)


def attention_kernel(
    node_ref, grad_ref, links_ref, table_ref, wq_ref, wkv_ref,
    attended_ref, send_ref, dnode_ref, weight_scr, dprob_scr,
):
    nodes, features = node_ref.shape
    degree = links_ref.shape[0]
    replicas = send_ref.shape[0]
    block = table_ref.shape[0] // replicas
    scale = 1.0 / math.sqrt(HEAD_DIM)
    node = node_ref[...]
    wkv = wkv_ref[...]
    queries = per_head(dot(node, wq_ref[...]).astype(BF16))
    upstream = per_head(grad_ref[...])
    q_heads, q_scaled = queries.astype(BF16), (queries * scale).astype(BF16)
    g_heads, g_scaled = upstream.astype(BF16), (upstream * scale).astype(BF16)

    links = links_ref[...]
    arrived = links >= replicas * nodes
    owner = jnp.where(arrived, links - replicas * nodes, links) // nodes
    links = owner * block + jnp.where(arrived, nodes, 0) + links % nodes

    keyval = []
    whole_kv = dot(table_ref[...], wkv).astype(BF16)
    total = jnp.zeros((1, HEADS * nodes), F32)
    inner = jnp.zeros((1, HEADS * nodes), F32)
    for r in range(replicas):
        span = slice(r * block, (r + 1) * block)
        kv = whole_kv[span, :]
        keyval.append(kv)
        here = (lax.broadcasted_iota(jnp.int32, (block, nodes), 0) + r * block).astype(jnp.int16)
        count = jnp.zeros((block, nodes), BF16)
        for j in range(degree):
            hit = here == jnp.broadcast_to(links[j : j + 1, :].astype(jnp.int16), here.shape)
            count = count + jnp.where(hit, jnp.ones_like(count), jnp.zeros_like(count))
        count = count.astype(F32)
        log_count = jnp.where(count > 0.0, jnp.log(jnp.maximum(count, 1.0)), -1e30)
        log_count = jnp.concatenate([log_count] * HEADS, 1)
        weight = jnp.exp(rows_of_both(kv[:, :features], q_scaled) + log_count)
        dprob = rows_of_both(kv[:, features:], g_scaled)
        total = total + jnp.sum(weight, axis=0, keepdims=True)
        inner = inner + jnp.sum(weight * dprob, axis=0, keepdims=True)
        weight_scr[span, :] = weight
        dprob_scr[span, :] = dprob

    inverse = 1.0 / total
    mean = inner * inverse
    attended = jnp.zeros((features, 2 * nodes), F32)
    dquery = jnp.zeros((features, 2 * nodes), F32)
    all_dkv = []
    for r in range(replicas):
        span = slice(r * block, (r + 1) * block)
        kv = keyval[r]
        prob = weight_scr[span, :] * inverse
        dscore = (prob * (dprob_scr[span, :] - mean)).astype(BF16)
        prob = prob.astype(BF16)
        attended = attended + per_pair(kv[:, features:], prob)
        dquery = dquery + per_pair(kv[:, :features], dscore)
        dkv = jnp.concatenate([dot(dscore, q_heads), dot(prob, g_heads)], 1).astype(BF16)
        all_dkv.append(dkv)
        dsrc = rows_of_both(dkv, wkv).astype(BF16)
        for part in range(2):
            for half in range(2):
                at = (part * 2 + half) * nodes
                send_ref[r, at : at + nodes, :] = dsrc[
                    part * nodes : (part + 1) * nodes, half * LANES : (half + 1) * LANES
                ]

    grad_kv = columns_of_both(table_ref[...], jnp.concatenate(all_dkv, 0))
    attended_ref[...] = own_blocks(attended, nodes).astype(BF16)
    dquery = own_blocks(dquery, nodes).astype(BF16)
    dnode_ref[...] = rows_of_both(dquery, wq_ref[...])
    grads = jnp.concatenate([columns_of_both(node, dquery), grad_kv], 1).astype(BF16)
    pieces = features * grads.shape[1] // (LANES * LANES)
    each = pieces // replicas
    down = features // LANES
    for piece in range(pieces):
        column, row = (piece // down) * LANES, (piece % down) * LANES
        at = 4 * nodes + (piece % each) * LANES
        send_ref[piece // each, at : at + LANES, :] = grads[row : row + LANES, column : column + LANES]


def attention(node_rows, grad_out, links, table, w_query, w_keyval, replicas):
    nodes, features = node_rows.shape
    entries = table.shape[0]
    sent = 4 * nodes + features * (features + w_keyval.shape[1]) // LANES // replicas
    whole = pl.BlockSpec(memory_space=pltpu.VMEM)
    return pl.pallas_call(
        attention_kernel,
        out_shape=(
            jax.ShapeDtypeStruct((nodes, features), BF16),
            jax.ShapeDtypeStruct((replicas, sent, LANES), BF16),
            jax.ShapeDtypeStruct((nodes, features), F32),
        ),
        in_specs=[whole] * 6,
        out_specs=(whole,) * 3,
        scratch_shapes=[pltpu.VMEM((entries, HEADS * nodes), F32)] * 2,
        compiler_params=pltpu.CompilerParams(vmem_limit_bytes=48 * 1024 * 1024),
        name="attention",
    )(node_rows, grad_out, links, table, w_query, w_keyval)


def shards(node_rows, w_query, w_keyval, need_rows, neighbours, grad_out):
    nodes, features = node_rows.shape
    ny, nz, nc, replicas = (lax.axis_size(a) for a in ("y", "z", "c", "x"))
    inner = nz * nc
    owners = ny * inner

    wanted = need_rows.reshape(owners, replicas).T
    my_rows = lax.dynamic_index_in_dim(wanted, lax.axis_index("x"), 0, keepdims=False)
    my_rows = my_rows[None, :]
    whole = pl.BlockSpec(memory_space=pltpu.VMEM)
    outgoing, kept = pl.pallas_call(
        pick_kernel,
        out_shape=(
            jax.ShapeDtypeStruct((owners, features), BF16),
            jax.ShapeDtypeStruct((nodes, features), BF16),
        ),
        in_specs=[whole] * 2,
        out_specs=(whole,) * 2,
        compiler_params=pltpu.CompilerParams(vmem_limit_bytes=SMALL),
        name="pick",
    )(my_rows, node_rows)
    incoming = exchange(outgoing.reshape(owners, -1, LANES), ("y", "z", "c")).reshape(owners, features)
    table = spread(jnp.concatenate([kept, incoming], 0), "x", replicas)
    table = table.reshape(-1, features)

    attended, partial, dnode = attention(
        kept, grad_out, neighbours.T, table, w_query, w_keyval, replicas
    )

    summed = jnp.sum(exchange(partial, "x").astype(F32), 0)
    back = summed[2 * nodes : 4 * nodes].astype(BF16).reshape(2, ny, nz, nc, LANES)
    grads = summed[4 * nodes :].astype(BF16).reshape(inner, -1, LANES)
    each = grads.shape[1]
    back = back.transpose(3, 2, 0, 1, 4).reshape(inner, 2 * ny, LANES)
    landed = exchange(jnp.concatenate([back, grads], 1), ("c", "z"))
    back = landed[:, : 2 * ny].reshape(inner, 2, ny, LANES).transpose(2, 1, 0, 3)
    back = back.reshape(ny, 2 * inner, LANES)
    grads = jnp.sum(landed[:, 2 * ny :].astype(F32), 0).astype(BF16)
    grads = jnp.broadcast_to(grads[None], (ny, each, LANES))
    landed = exchange(jnp.concatenate([back, grads], 1), "y")
    grads = jnp.sum(landed[:, 2 * inner :].astype(F32), 0).astype(BF16)
    grads = spread(grads, ("x", "z"), nz * replicas)
    grads = grads.reshape(replicas, nz, each, LANES)
    other = lax.ppermute(grads, "c", [(0, 1), (1, 0)])
    core = lax.axis_index("c").reshape(1)
    return pl.pallas_call(
        finish_kernel,
        out_shape=(
            jax.ShapeDtypeStruct((nodes, features), BF16),
            jax.ShapeDtypeStruct((nodes, features), BF16),
            jax.ShapeDtypeStruct(w_query.shape, F32),
            jax.ShapeDtypeStruct(w_keyval.shape, F32),
        ),
        in_specs=[pl.BlockSpec(memory_space=pltpu.SMEM)] + [whole] * 7,
        out_specs=(whole,) * 4,
        compiler_params=pltpu.CompilerParams(vmem_limit_bytes=SMALL),
        name="finish",
    )(core, my_rows, landed, summed, dnode, grads, other, attended)


def solution(mesh):
    own, rep = mesh.devices.shape
    side = math.isqrt(own // 2)
    fine = Mesh(mesh.devices.reshape(side, own // 2 // side, 2, rep), ("y", "z", "c", "x"))
    rows = P(("y", "z", "c", "x"), None)
    in_specs = (rows, P(), P(), P(None, ("y", "z", "c"), None, None), rows, rows)
    return jax.shard_map(
        shards, mesh=fine, in_specs=in_specs, out_specs=(rows, rows, P(), P()), check_vma=False
    )
```

```python
import itertools
import math

import jax
import jax.numpy as jnp
from jax import lax
from jax.experimental import pallas as pl
from jax.experimental.pallas import tpu as pltpu
from jax.sharding import Mesh
from jax.sharding import PartitionSpec as P

HEADS = 4
HEAD_DIM = 64
LANES = 128
CORES = 2
SMALL = 8 * 1024 * 1024
BF16, F32 = jnp.bfloat16, jnp.float32


def dot(a, b, contract=((1,), (0,))):
    return lax.dot_general(a, b, (contract, ((), ())), preferred_element_type=F32)


def rows_of_both(a, b):
    return dot(a, b, ((1,), (1,)))


def columns_of_both(a, b):
    return dot(a, b, ((0,), (0,)))


def exchange(blocks, axes):
    return lax.all_to_all(blocks, axes, split_axis=0, concat_axis=0, tiled=True)


def spread(block, axes, count):
    return exchange(jnp.broadcast_to(block[None], (count,) + block.shape), axes)


def per_head(rows):
    head = lax.broadcasted_iota(jnp.int32, rows.shape, 1) // HEAD_DIM
    wide = rows.astype(F32)
    return jnp.concatenate([jnp.where(head == h, wide, 0.0) for h in range(HEADS)], 0)


def per_pair(values, weights):
    wide, long = weights.shape[1] // (HEADS // 2), 2 * HEAD_DIM
    pairs = [
        columns_of_both(values[:, p * long : (p + 1) * long], weights[:, p * wide : (p + 1) * wide])
        for p in range(HEADS // 2)
    ]
    return jnp.concatenate(pairs, 0)


def own_blocks(table, nodes):
    blocks = [
        table[h * HEAD_DIM : (h + 1) * HEAD_DIM, h % 2 * nodes : (h % 2 + 1) * nodes]
        for h in range(HEADS)
    ]
    return jnp.concatenate(blocks, 0).T


def pick_kernel(rows_ref, node_ref, out_ref, kept_ref):
    kept_ref[...] = node_ref[...]
    nodes = node_ref.shape[0]
    picks = lax.broadcasted_iota(jnp.int32, (nodes, rows_ref.shape[1]), 0) == rows_ref[...]
    picks = jnp.where(picks, 1.0, 0.0).astype(BF16)
    out_ref[...] = columns_of_both(picks, node_ref[...]).astype(BF16)


def node_kernel(rows_ref, landed_ref, summed_ref, dnode_ref, attended_in_ref, attended_ref, nodes_ref):
    nodes, features = dnode_ref.shape
    outer, _, lanes = landed_ref.shape
    owners = rows_ref.shape[1]
    inner = owners // outer
    depth = inner // CORES
    attended_ref[...] = attended_in_ref[...]
    picks = lax.broadcasted_iota(jnp.int32, (nodes, owners), 0) == rows_ref[...]
    picks = jnp.where(picks, 1.0, 0.0).astype(BF16)
    given = lax.broadcasted_iota(jnp.int32, (owners, owners), 0)
    asked = lax.broadcasted_iota(jnp.int32, (owners, owners), 1)
    asked = asked // inner * inner + asked % depth * CORES + asked // depth % CORES
    picks = dot(picks, jnp.where(given == asked, 1.0, 0.0).astype(BF16)).astype(BF16)
    for half in range(features // LANES):
        at = slice(half * LANES, (half + 1) * LANES)
        back = landed_ref[:, half * inner : (half + 1) * inner, :].reshape(owners, lanes)
        total = summed_ref[half * nodes : (half + 1) * nodes, :] + dnode_ref[:, at]
        nodes_ref[:, at] = (total + dot(picks, back)).astype(BF16)


def weight_kernel(core_ref, mine_ref, other_ref, grad_q_ref, grad_kv_ref):
    features = grad_q_ref.shape[0]
    replicas, depth, each, _ = mine_ref.shape
    for x, z, c in itertools.product(range(replicas), range(depth), range(CORES)):
        block = jnp.where(core_ref[0] == c, mine_ref[x, z], other_ref[x, z]).astype(F32)
        first = ((x * CORES + c) * depth + z) * each
        for row in range(first, first + each, 8):
            column, at = row // features * LANES, row % features
            to_ref = grad_q_ref if column < features else grad_kv_ref
            column = column if column < features else column - features
            to_ref[at : at + 8, column : column + LANES] = block[row - first : row - first + 8]


def attention_kernel(
    node_ref, grad_ref, links_ref, table_ref, wq_ref, wkv_ref,
    attended_ref, send_ref, dnode_ref, weight_scr, dprob_scr,
):
    nodes, features = node_ref.shape
    degree = links_ref.shape[0]
    replicas = send_ref.shape[0]
    block = table_ref.shape[0] // replicas
    scale = 1.0 / math.sqrt(HEAD_DIM)
    node = node_ref[...]
    wkv = wkv_ref[...]
    queries = per_head(dot(node, wq_ref[...]).astype(BF16))
    upstream = per_head(grad_ref[...])
    q_heads, q_scaled = queries.astype(BF16), (queries * scale).astype(BF16)
    g_heads, g_scaled = upstream.astype(BF16), (upstream * scale).astype(BF16)

    links = links_ref[...]
    arrived = links >= replicas * nodes
    owner = jnp.where(arrived, links - replicas * nodes, links) // nodes
    links = owner * block + jnp.where(arrived, nodes, 0) + links % nodes

    keyval = []
    whole_kv = dot(table_ref[...], wkv).astype(BF16)
    total = jnp.zeros((1, HEADS * nodes), F32)
    inner = jnp.zeros((1, HEADS * nodes), F32)
    for r in range(replicas):
        span = slice(r * block, (r + 1) * block)
        kv = whole_kv[span, :]
        keyval.append(kv)
        here = (lax.broadcasted_iota(jnp.int32, (block, nodes), 0) + r * block).astype(jnp.int16)
        count = jnp.zeros((block, nodes), BF16)
        for j in range(degree):
            hit = here == jnp.broadcast_to(links[j : j + 1, :].astype(jnp.int16), here.shape)
            count = count + jnp.where(hit, jnp.ones_like(count), jnp.zeros_like(count))
        count = count.astype(F32)
        log_count = jnp.where(count > 0.0, jnp.log(jnp.maximum(count, 1.0)), -1e30)
        log_count = jnp.concatenate([log_count] * HEADS, 1)
        weight = jnp.exp(rows_of_both(kv[:, :features], q_scaled) + log_count)
        dprob = rows_of_both(kv[:, features:], g_scaled)
        total = total + jnp.sum(weight, axis=0, keepdims=True)
        inner = inner + jnp.sum(weight * dprob, axis=0, keepdims=True)
        weight_scr[span, :] = weight
        dprob_scr[span, :] = dprob

    inverse = 1.0 / total
    mean = inner * inverse
    attended = jnp.zeros((features, 2 * nodes), F32)
    dquery = jnp.zeros((features, 2 * nodes), F32)
    all_dkv = []
    for r in range(replicas):
        span = slice(r * block, (r + 1) * block)
        kv = keyval[r]
        prob = weight_scr[span, :] * inverse
        dscore = (prob * (dprob_scr[span, :] - mean)).astype(BF16)
        prob = prob.astype(BF16)
        attended = attended + per_pair(kv[:, features:], prob)
        dquery = dquery + per_pair(kv[:, :features], dscore)
        dkv = jnp.concatenate([dot(dscore, q_heads), dot(prob, g_heads)], 1).astype(BF16)
        all_dkv.append(dkv)
        dsrc = rows_of_both(dkv, wkv).astype(BF16)
        for part in range(2):
            for half in range(2):
                at = (part * 2 + half) * nodes
                send_ref[r, at : at + nodes, :] = dsrc[
                    part * nodes : (part + 1) * nodes, half * LANES : (half + 1) * LANES
                ]

    grad_kv = columns_of_both(table_ref[...], jnp.concatenate(all_dkv, 0))
    attended_ref[...] = own_blocks(attended, nodes).astype(BF16)
    dquery = own_blocks(dquery, nodes).astype(BF16)
    dnode_ref[...] = rows_of_both(dquery, wq_ref[...])
    grads = jnp.concatenate([columns_of_both(node, dquery), grad_kv], 1).astype(BF16)
    pieces = features * grads.shape[1] // (LANES * LANES)
    each = pieces // replicas
    down = features // LANES
    for piece in range(pieces):
        column, row = (piece // down) * LANES, (piece % down) * LANES
        at = 4 * nodes + (piece % each) * LANES
        send_ref[piece // each, at : at + LANES, :] = grads[row : row + LANES, column : column + LANES]


def attention(node_rows, grad_out, links, table, w_query, w_keyval, replicas):
    nodes, features = node_rows.shape
    entries = table.shape[0]
    sent = 4 * nodes + features * (features + w_keyval.shape[1]) // LANES // replicas
    whole = pl.BlockSpec(memory_space=pltpu.VMEM)
    return pl.pallas_call(
        attention_kernel,
        out_shape=(
            jax.ShapeDtypeStruct((nodes, features), BF16),
            jax.ShapeDtypeStruct((replicas, sent, LANES), BF16),
            jax.ShapeDtypeStruct((nodes, features), F32),
        ),
        in_specs=[whole] * 6,
        out_specs=(whole,) * 3,
        scratch_shapes=[pltpu.VMEM((entries, HEADS * nodes), F32)] * 2,
        compiler_params=pltpu.CompilerParams(vmem_limit_bytes=48 * 1024 * 1024),
        name="attention",
    )(node_rows, grad_out, links, table, w_query, w_keyval)


def shards(node_rows, w_query, w_keyval, need_rows, neighbours, grad_out):
    nodes, features = node_rows.shape
    ny, nz, nc, replicas = (lax.axis_size(a) for a in ("y", "z", "c", "x"))
    inner = nz * nc
    owners = ny * inner

    wanted = need_rows.reshape(owners, replicas).T
    my_rows = lax.dynamic_index_in_dim(wanted, lax.axis_index("x"), 0, keepdims=False)
    my_rows = my_rows[None, :]
    whole = pl.BlockSpec(memory_space=pltpu.VMEM)
    outgoing, kept = pl.pallas_call(
        pick_kernel,
        out_shape=(
            jax.ShapeDtypeStruct((owners, features), BF16),
            jax.ShapeDtypeStruct((nodes, features), BF16),
        ),
        in_specs=[whole] * 2,
        out_specs=(whole,) * 2,
        compiler_params=pltpu.CompilerParams(vmem_limit_bytes=SMALL),
        name="pick",
    )(my_rows, node_rows)
    incoming = exchange(outgoing.reshape(owners, -1, LANES), ("y", "z", "c")).reshape(owners, features)
    table = lax.all_gather(jnp.concatenate([kept, incoming], 0), "x", axis=0, tiled=True)

    attended, partial, dnode = attention(
        kept, grad_out, neighbours.T, table, w_query, w_keyval, replicas
    )

    summed = jnp.sum(exchange(partial, "x").astype(F32), 0)
    back = summed[2 * nodes : 4 * nodes].astype(BF16).reshape(2, ny, nz, nc, LANES)
    grads = summed[4 * nodes :].astype(BF16).reshape(inner, -1, LANES)
    each = grads.shape[1]
    back = back.transpose(3, 2, 0, 1, 4).reshape(inner, 2 * ny, LANES)
    landed = exchange(jnp.concatenate([back, grads], 1), ("c", "z"))
    back = landed[:, : 2 * ny].reshape(inner, 2, ny, LANES).transpose(2, 1, 0, 3)
    back = back.reshape(ny, 2 * inner, LANES)
    grads = jnp.sum(landed[:, 2 * ny :].astype(F32), 0).astype(BF16)
    grads = jnp.broadcast_to(grads[None], (ny, each, LANES))
    landed = exchange(jnp.concatenate([back, grads], 1), "y")
    grads = jnp.sum(landed[:, 2 * inner :].astype(F32), 0).astype(BF16)
    grads = spread(grads, ("x", "z"), nz * replicas)
    grads = grads.reshape(replicas, nz, each, LANES)
    other = lax.ppermute(grads, "c", [(0, 1), (1, 0)])
    core = lax.axis_index("c").reshape(1)
    attended, grad_nodes = pl.pallas_call(
        node_kernel,
        out_shape=(jax.ShapeDtypeStruct((nodes, features), BF16),) * 2,
        in_specs=[whole] * 5,
        out_specs=(whole,) * 2,
        compiler_params=pltpu.CompilerParams(vmem_limit_bytes=SMALL),
        name="node_sums",
    )(my_rows, landed, summed, dnode, attended)
    grad_query, grad_keyval = pl.pallas_call(
        weight_kernel,
        out_shape=(
            jax.ShapeDtypeStruct(w_query.shape, F32),
            jax.ShapeDtypeStruct(w_keyval.shape, F32),
        ),
        in_specs=[pl.BlockSpec(memory_space=pltpu.SMEM)] + [whole] * 2,
        out_specs=(whole,) * 2,
        compiler_params=pltpu.CompilerParams(vmem_limit_bytes=SMALL),
        name="weight_gradients",
    )(core, grads, other)
    return attended, grad_nodes, grad_query, grad_keyval


def solution(mesh):
    own, rep = mesh.devices.shape
    side = math.isqrt(own // 2)
    fine = Mesh(mesh.devices.reshape(side, own // 2 // side, 2, rep), ("y", "z", "c", "x"))
    rows = P(("y", "z", "c", "x"), None)
    in_specs = (rows, P(), P(), P(None, ("y", "z", "c"), None, None), rows, rows)
    return jax.shard_map(
        shards, mesh=fine, in_specs=in_specs, out_specs=(rows, rows, P(), P()), check_vma=False
    )
```

```python
import itertools
import math

import jax
import jax.numpy as jnp
from jax import lax
from jax.experimental import pallas as pl
from jax.experimental.pallas import tpu as pltpu
from jax.sharding import Mesh
from jax.sharding import PartitionSpec as P

HEADS = 4
HEAD_DIM = 64
LANES = 128
CORES = 2
SMALL = 8 * 1024 * 1024
BF16, F32 = jnp.bfloat16, jnp.float32


def dot(a, b, contract=((1,), (0,))):
    return lax.dot_general(a, b, (contract, ((), ())), preferred_element_type=F32)


def rows_of_both(a, b):
    return dot(a, b, ((1,), (1,)))


def columns_of_both(a, b):
    return dot(a, b, ((0,), (0,)))


def exchange(blocks, axes):
    return lax.all_to_all(blocks, axes, split_axis=0, concat_axis=0, tiled=True)


def spread(block, axes, count):
    return exchange(jnp.broadcast_to(block[None], (count,) + block.shape), axes)


def per_head(rows):
    head = lax.broadcasted_iota(jnp.int32, rows.shape, 1) // HEAD_DIM
    wide = rows.astype(F32)
    return jnp.concatenate([jnp.where(head == h, wide, 0.0) for h in range(HEADS)], 0)


def per_pair(values, weights):
    wide, long = weights.shape[1] // (HEADS // 2), 2 * HEAD_DIM
    pairs = [
        columns_of_both(values[:, p * long : (p + 1) * long], weights[:, p * wide : (p + 1) * wide])
        for p in range(HEADS // 2)
    ]
    return jnp.concatenate(pairs, 0)


def own_blocks(table, nodes):
    blocks = [
        table[h * HEAD_DIM : (h + 1) * HEAD_DIM, h % 2 * nodes : (h % 2 + 1) * nodes]
        for h in range(HEADS)
    ]
    return jnp.concatenate(blocks, 0).T


def keep_kernel(node_ref, kept_ref):
    kept_ref[...] = node_ref[...]


def pick_kernel(rows_ref, node_ref, out_ref):
    nodes = node_ref.shape[0]
    picks = lax.broadcasted_iota(jnp.int32, (nodes, rows_ref.shape[1]), 0) == rows_ref[...]
    picks = jnp.where(picks, 1.0, 0.0).astype(BF16)
    out_ref[...] = columns_of_both(picks, node_ref[...]).astype(BF16)


def node_kernel(rows_ref, landed_ref, summed_ref, dnode_ref, attended_in_ref, attended_ref, nodes_ref):
    nodes, features = dnode_ref.shape
    outer, _, lanes = landed_ref.shape
    owners = rows_ref.shape[1]
    inner = owners // outer
    depth = inner // CORES
    attended_ref[...] = attended_in_ref[...]
    picks = lax.broadcasted_iota(jnp.int32, (nodes, owners), 0) == rows_ref[...]
    picks = jnp.where(picks, 1.0, 0.0).astype(BF16)
    given = lax.broadcasted_iota(jnp.int32, (owners, owners), 0)
    asked = lax.broadcasted_iota(jnp.int32, (owners, owners), 1)
    asked = asked // inner * inner + asked % depth * CORES + asked // depth % CORES
    picks = dot(picks, jnp.where(given == asked, 1.0, 0.0).astype(BF16)).astype(BF16)
    for half in range(features // LANES):
        at = slice(half * LANES, (half + 1) * LANES)
        back = landed_ref[:, half * inner : (half + 1) * inner, :].reshape(owners, lanes)
        total = summed_ref[half * nodes : (half + 1) * nodes, :] + dnode_ref[:, at]
        nodes_ref[:, at] = (total + dot(picks, back)).astype(BF16)


def weight_kernel(core_ref, mine_ref, other_ref, grad_q_ref, grad_kv_ref):
    features = grad_q_ref.shape[0]
    replicas, depth, each, _ = mine_ref.shape
    for x, z, c in itertools.product(range(replicas), range(depth), range(CORES)):
        block = jnp.where(core_ref[0] == c, mine_ref[x, z], other_ref[x, z]).astype(F32)
        first = ((x * CORES + c) * depth + z) * each
        for row in range(first, first + each, 8):
            column, at = row // features * LANES, row % features
            to_ref = grad_q_ref if column < features else grad_kv_ref
            column = column if column < features else column - features
            to_ref[at : at + 8, column : column + LANES] = block[row - first : row - first + 8]


def attention_kernel(
    node_ref, grad_ref, links_ref, table_ref, wq_ref, wkv_ref,
    attended_ref, send_ref, dnode_ref, weight_scr, dprob_scr,
):
    nodes, features = node_ref.shape
    degree = links_ref.shape[0]
    replicas = send_ref.shape[0]
    block = table_ref.shape[0] // replicas
    scale = 1.0 / math.sqrt(HEAD_DIM)
    node = node_ref[...]
    wkv = wkv_ref[...]
    queries = per_head(dot(node, wq_ref[...]).astype(BF16))
    upstream = per_head(grad_ref[...])
    q_heads, q_scaled = queries.astype(BF16), (queries * scale).astype(BF16)
    g_heads, g_scaled = upstream.astype(BF16), (upstream * scale).astype(BF16)

    links = links_ref[...]
    arrived = links >= replicas * nodes
    owner = jnp.where(arrived, links - replicas * nodes, links) // nodes
    links = owner * block + jnp.where(arrived, nodes, 0) + links % nodes

    keyval = []
    whole_kv = dot(table_ref[...], wkv).astype(BF16)
    total = jnp.zeros((1, HEADS * nodes), F32)
    inner = jnp.zeros((1, HEADS * nodes), F32)
    for r in range(replicas):
        span = slice(r * block, (r + 1) * block)
        kv = whole_kv[span, :]
        keyval.append(kv)
        here = (lax.broadcasted_iota(jnp.int32, (block, nodes), 0) + r * block).astype(jnp.int16)
        count = jnp.zeros((block, nodes), BF16)
        for j in range(degree):
            hit = here == jnp.broadcast_to(links[j : j + 1, :].astype(jnp.int16), here.shape)
            count = count + jnp.where(hit, jnp.ones_like(count), jnp.zeros_like(count))
        count = count.astype(F32)
        log_count = jnp.where(count > 0.0, jnp.log(jnp.maximum(count, 1.0)), -1e30)
        log_count = jnp.concatenate([log_count] * HEADS, 1)
        weight = jnp.exp(rows_of_both(kv[:, :features], q_scaled) + log_count)
        dprob = rows_of_both(kv[:, features:], g_scaled)
        total = total + jnp.sum(weight, axis=0, keepdims=True)
        inner = inner + jnp.sum(weight * dprob, axis=0, keepdims=True)
        weight_scr[span, :] = weight
        dprob_scr[span, :] = dprob

    inverse = 1.0 / total
    mean = inner * inverse
    attended = jnp.zeros((features, 2 * nodes), F32)
    dquery = jnp.zeros((features, 2 * nodes), F32)
    all_dkv = []
    for r in range(replicas):
        span = slice(r * block, (r + 1) * block)
        kv = keyval[r]
        prob = weight_scr[span, :] * inverse
        dscore = (prob * (dprob_scr[span, :] - mean)).astype(BF16)
        prob = prob.astype(BF16)
        attended = attended + per_pair(kv[:, features:], prob)
        dquery = dquery + per_pair(kv[:, :features], dscore)
        dkv = jnp.concatenate([dot(dscore, q_heads), dot(prob, g_heads)], 1).astype(BF16)
        all_dkv.append(dkv)
        dsrc = rows_of_both(dkv, wkv).astype(BF16)
        for part in range(2):
            for half in range(2):
                at = (part * 2 + half) * nodes
                send_ref[r, at : at + nodes, :] = dsrc[
                    part * nodes : (part + 1) * nodes, half * LANES : (half + 1) * LANES
                ]

    grad_kv = columns_of_both(table_ref[...], jnp.concatenate(all_dkv, 0))
    attended_ref[...] = own_blocks(attended, nodes).astype(BF16)
    dquery = own_blocks(dquery, nodes).astype(BF16)
    dnode_ref[...] = rows_of_both(dquery, wq_ref[...])
    grads = jnp.concatenate([columns_of_both(node, dquery), grad_kv], 1).astype(BF16)
    pieces = features * grads.shape[1] // (LANES * LANES)
    each = pieces // replicas
    down = features // LANES
    for piece in range(pieces):
        column, row = (piece // down) * LANES, (piece % down) * LANES
        at = 4 * nodes + (piece % each) * LANES
        send_ref[piece // each, at : at + LANES, :] = grads[row : row + LANES, column : column + LANES]


def attention(node_rows, grad_out, links, table, w_query, w_keyval, replicas):
    nodes, features = node_rows.shape
    entries = table.shape[0]
    sent = 4 * nodes + features * (features + w_keyval.shape[1]) // LANES // replicas
    whole = pl.BlockSpec(memory_space=pltpu.VMEM)
    return pl.pallas_call(
        attention_kernel,
        out_shape=(
            jax.ShapeDtypeStruct((nodes, features), BF16),
            jax.ShapeDtypeStruct((replicas, sent, LANES), BF16),
            jax.ShapeDtypeStruct((nodes, features), F32),
        ),
        in_specs=[whole] * 6,
        out_specs=(whole,) * 3,
        scratch_shapes=[pltpu.VMEM((entries, HEADS * nodes), F32)] * 2,
        compiler_params=pltpu.CompilerParams(vmem_limit_bytes=48 * 1024 * 1024),
        name="attention",
    )(node_rows, grad_out, links, table, w_query, w_keyval)


def shards(node_rows, w_query, w_keyval, need_rows, neighbours, grad_out):
    nodes, features = node_rows.shape
    ny, nz, nc, replicas = (lax.axis_size(a) for a in ("y", "z", "c", "x"))
    inner = nz * nc
    owners = ny * inner

    whole = pl.BlockSpec(memory_space=pltpu.VMEM)
    small = pltpu.CompilerParams(vmem_limit_bytes=SMALL)
    rows = jax.ShapeDtypeStruct((nodes, features), BF16)
    kept = pl.pallas_call(
        keep_kernel,
        out_shape=rows,
        in_specs=[whole],
        out_specs=whole,
        compiler_params=small,
        name="keep",
    )(node_rows)
    need_rows, kept = lax.optimization_barrier((need_rows, kept))
    wanted = need_rows.reshape(owners, replicas).T
    my_rows = lax.dynamic_index_in_dim(wanted, lax.axis_index("x"), 0, keepdims=False)
    my_rows = my_rows[None, :]
    outgoing = pl.pallas_call(
        pick_kernel,
        out_shape=jax.ShapeDtypeStruct((owners, features), BF16),
        in_specs=[whole] * 2,
        out_specs=whole,
        compiler_params=small,
        name="pick",
    )(my_rows, kept)
    incoming = exchange(outgoing.reshape(owners, -1, LANES), ("y", "z", "c")).reshape(owners, features)
    table = lax.all_gather(jnp.concatenate([kept, incoming], 0), "x", axis=0, tiled=True)

    attended, partial, dnode = attention(
        kept, grad_out, neighbours.T, table, w_query, w_keyval, replicas
    )

    summed = jnp.sum(exchange(partial, "x").astype(F32), 0)
    back = summed[2 * nodes : 4 * nodes].astype(BF16).reshape(2, ny, nz, nc, LANES)
    grads = summed[4 * nodes :].astype(BF16).reshape(inner, -1, LANES)
    each = grads.shape[1]
    back = back.transpose(3, 2, 0, 1, 4).reshape(inner, 2 * ny, LANES)
    landed = exchange(jnp.concatenate([back, grads], 1), ("c", "z"))
    back = landed[:, : 2 * ny].reshape(inner, 2, ny, LANES).transpose(2, 1, 0, 3)
    back = back.reshape(ny, 2 * inner, LANES)
    grads = jnp.sum(landed[:, 2 * ny :].astype(F32), 0).astype(BF16)
    grads = jnp.broadcast_to(grads[None], (ny, each, LANES))
    landed = exchange(jnp.concatenate([back, grads], 1), "y")
    grads = jnp.sum(landed[:, 2 * inner :].astype(F32), 0).astype(BF16)
    grads = spread(grads, ("x", "z"), nz * replicas)
    grads = grads.reshape(replicas, nz, each, LANES)
    other = lax.ppermute(grads, "c", [(0, 1), (1, 0)])
    core = lax.axis_index("c").reshape(1)
    attended, grad_nodes = pl.pallas_call(
        node_kernel,
        out_shape=(jax.ShapeDtypeStruct((nodes, features), BF16),) * 2,
        in_specs=[whole] * 5,
        out_specs=(whole,) * 2,
        compiler_params=pltpu.CompilerParams(vmem_limit_bytes=SMALL),
        name="node_sums",
    )(my_rows, landed, summed, dnode, attended)
    grad_query, grad_keyval = pl.pallas_call(
        weight_kernel,
        out_shape=(
            jax.ShapeDtypeStruct(w_query.shape, F32),
            jax.ShapeDtypeStruct(w_keyval.shape, F32),
        ),
        in_specs=[pl.BlockSpec(memory_space=pltpu.SMEM)] + [whole] * 2,
        out_specs=(whole,) * 2,
        compiler_params=pltpu.CompilerParams(vmem_limit_bytes=SMALL),
        name="weight_gradients",
    )(core, grads, other)
    return attended, grad_nodes, grad_query, grad_keyval


def solution(mesh):
    own, rep = mesh.devices.shape
    side = math.isqrt(own // 2)
    fine = Mesh(mesh.devices.reshape(side, own // 2 // side, 2, rep), ("y", "z", "c", "x"))
    rows = P(("y", "z", "c", "x"), None)
    in_specs = (rows, P(), P(), P(None, ("y", "z", "c"), None, None), rows, rows)
    return jax.shard_map(
        shards, mesh=fine, in_specs=in_specs, out_specs=(rows, rows, P(), P()), check_vma=False
    )
```

```python
import itertools
import math

import jax
import jax.numpy as jnp
from jax import lax
from jax.experimental import pallas as pl
from jax.experimental.pallas import tpu as pltpu
from jax.sharding import Mesh
from jax.sharding import PartitionSpec as P

HEADS = 4
HEAD_DIM = 64
LANES = 128
CORES = 2
SMALL = 8 * 1024 * 1024
BF16, F32 = jnp.bfloat16, jnp.float32


def dot(a, b, contract=((1,), (0,))):
    return lax.dot_general(a, b, (contract, ((), ())), preferred_element_type=F32)


def rows_of_both(a, b):
    return dot(a, b, ((1,), (1,)))


def columns_of_both(a, b):
    return dot(a, b, ((0,), (0,)))


def exchange(blocks, axes):
    return lax.all_to_all(blocks, axes, split_axis=0, concat_axis=0, tiled=True)


def spread(block, axes, count):
    return exchange(jnp.broadcast_to(block[None], (count,) + block.shape), axes)


def per_head(rows):
    head = lax.broadcasted_iota(jnp.int32, rows.shape, 1) // HEAD_DIM
    wide = rows.astype(F32)
    return jnp.concatenate([jnp.where(head == h, wide, 0.0) for h in range(HEADS)], 0)


def per_pair(values, weights):
    wide, long = weights.shape[1] // (HEADS // 2), 2 * HEAD_DIM
    pairs = [
        columns_of_both(values[:, p * long : (p + 1) * long], weights[:, p * wide : (p + 1) * wide])
        for p in range(HEADS // 2)
    ]
    return jnp.concatenate(pairs, 0)


def own_blocks(table, nodes):
    blocks = [
        table[h * HEAD_DIM : (h + 1) * HEAD_DIM, h % 2 * nodes : (h % 2 + 1) * nodes]
        for h in range(HEADS)
    ]
    return jnp.concatenate(blocks, 0).T


def keep_kernel(node_ref, kept_ref):
    kept_ref[...] = node_ref[...]


def pick_kernel(rows_ref, node_ref, out_ref):
    nodes = node_ref.shape[0]
    picks = lax.broadcasted_iota(jnp.int32, (nodes, rows_ref.shape[1]), 0) == rows_ref[...]
    picks = jnp.where(picks, 1.0, 0.0).astype(BF16)
    out_ref[...] = columns_of_both(picks, node_ref[...]).astype(BF16)


def node_kernel(rows_ref, landed_ref, summed_ref, dnode_ref, attended_in_ref, attended_ref, nodes_ref):
    nodes, features = dnode_ref.shape
    outer, _, lanes = landed_ref.shape
    owners = rows_ref.shape[1]
    inner = owners // outer
    depth = inner // CORES
    attended_ref[...] = attended_in_ref[...]
    picks = lax.broadcasted_iota(jnp.int32, (nodes, owners), 0) == rows_ref[...]
    picks = jnp.where(picks, 1.0, 0.0).astype(BF16)
    given = lax.broadcasted_iota(jnp.int32, (owners, owners), 0)
    asked = lax.broadcasted_iota(jnp.int32, (owners, owners), 1)
    asked = asked // inner * inner + asked % depth * CORES + asked // depth % CORES
    picks = dot(picks, jnp.where(given == asked, 1.0, 0.0).astype(BF16)).astype(BF16)
    for half in range(features // LANES):
        at = slice(half * LANES, (half + 1) * LANES)
        back = landed_ref[:, half * inner : (half + 1) * inner, :].reshape(owners, lanes)
        total = summed_ref[half * nodes : (half + 1) * nodes, :] + dnode_ref[:, at]
        nodes_ref[:, at] = (total + dot(picks, back)).astype(BF16)


def weight_kernel(core_ref, mine_ref, other_ref, grad_q_ref, grad_kv_ref):
    features = grad_q_ref.shape[0]
    replicas, depth, each, _ = mine_ref.shape
    for x, z, c in itertools.product(range(replicas), range(depth), range(CORES)):
        block = jnp.where(core_ref[0] == c, mine_ref[x, z], other_ref[x, z]).astype(F32)
        first = ((x * CORES + c) * depth + z) * each
        for row in range(first, first + each, 8):
            column, at = row // features * LANES, row % features
            to_ref = grad_q_ref if column < features else grad_kv_ref
            column = column if column < features else column - features
            to_ref[at : at + 8, column : column + LANES] = block[row - first : row - first + 8]


def attention_kernel(
    node_ref, grad_ref, links_ref, table_ref, wq_ref, wkv_ref,
    attended_ref, send_ref, dnode_ref, weight_scr, dprob_scr,
):
    nodes, features = node_ref.shape
    degree = links_ref.shape[0]
    replicas = send_ref.shape[0]
    block = table_ref.shape[0] // replicas
    scale = 1.0 / math.sqrt(HEAD_DIM)
    node = node_ref[...]
    wkv = wkv_ref[...]
    queries = per_head(dot(node, wq_ref[...]).astype(BF16))
    upstream = per_head(grad_ref[...])
    q_heads, q_scaled = queries.astype(BF16), (queries * scale).astype(BF16)
    g_heads, g_scaled = upstream.astype(BF16), (upstream * scale).astype(BF16)

    links = links_ref[...]
    arrived = links >= replicas * nodes
    owner = jnp.where(arrived, links - replicas * nodes, links) // nodes
    links = owner * block + jnp.where(arrived, nodes, 0) + links % nodes

    keyval = []
    whole_kv = dot(table_ref[...], wkv).astype(BF16)
    peaks, totals, inners = [], [], []
    for r in range(replicas):
        span = slice(r * block, (r + 1) * block)
        kv = whole_kv[span, :]
        keyval.append(kv)
        here = (lax.broadcasted_iota(jnp.int32, (block, nodes), 0) + r * block).astype(jnp.int16)
        count = jnp.zeros((block, nodes), BF16)
        for j in range(degree):
            hit = here == jnp.broadcast_to(links[j : j + 1, :].astype(jnp.int16), here.shape)
            count = count + jnp.where(hit, jnp.ones_like(count), jnp.zeros_like(count))
        count = count.astype(F32)
        log_count = jnp.where(count > 0.0, jnp.log(jnp.maximum(count, 1.0)), -1e30)
        log_count = jnp.concatenate([log_count] * HEADS, 1)
        score = rows_of_both(kv[:, :features], q_scaled) + log_count
        peaks.append(jnp.max(score, axis=0, keepdims=True))
        weight = jnp.exp(score - peaks[r])
        dprob = rows_of_both(kv[:, features:], g_scaled)
        totals.append(jnp.sum(weight, axis=0, keepdims=True))
        inners.append(jnp.sum(weight * dprob, axis=0, keepdims=True))
        weight_scr[span, :] = weight
        dprob_scr[span, :] = dprob

    peak = peaks[0]
    for other in peaks[1:]:
        peak = jnp.maximum(peak, other)
    factors = [jnp.exp(part - peak) for part in peaks]
    inverse = 1.0 / sum(f * t for f, t in zip(factors, totals))
    factors = [f * inverse for f in factors]
    mean = sum(f * t for f, t in zip(factors, inners))
    attended = jnp.zeros((features, 2 * nodes), F32)
    dquery = jnp.zeros((features, 2 * nodes), F32)
    all_dkv = []
    for r in range(replicas):
        span = slice(r * block, (r + 1) * block)
        kv = keyval[r]
        prob = weight_scr[span, :] * factors[r]
        dscore = (prob * (dprob_scr[span, :] - mean)).astype(BF16)
        prob = prob.astype(BF16)
        attended = attended + per_pair(kv[:, features:], prob)
        dquery = dquery + per_pair(kv[:, :features], dscore)
        dkv = jnp.concatenate([dot(dscore, q_heads), dot(prob, g_heads)], 1).astype(BF16)
        all_dkv.append(dkv)
        dsrc = rows_of_both(dkv, wkv).astype(BF16)
        for part in range(2):
            for half in range(2):
                at = (part * 2 + half) * nodes
                send_ref[r, at : at + nodes, :] = dsrc[
                    part * nodes : (part + 1) * nodes, half * LANES : (half + 1) * LANES
                ]

    grad_kv = columns_of_both(table_ref[...], jnp.concatenate(all_dkv, 0))
    attended_ref[...] = own_blocks(attended, nodes).astype(BF16)
    dquery = own_blocks(dquery, nodes).astype(BF16)
    dnode_ref[...] = rows_of_both(dquery, wq_ref[...])
    grads = jnp.concatenate([columns_of_both(node, dquery), grad_kv], 1).astype(BF16)
    pieces = features * grads.shape[1] // (LANES * LANES)
    each = pieces // replicas
    down = features // LANES
    for piece in range(pieces):
        column, row = (piece // down) * LANES, (piece % down) * LANES
        at = 4 * nodes + (piece % each) * LANES
        send_ref[piece // each, at : at + LANES, :] = grads[row : row + LANES, column : column + LANES]


def attention(node_rows, grad_out, links, table, w_query, w_keyval, replicas):
    nodes, features = node_rows.shape
    entries = table.shape[0]
    sent = 4 * nodes + features * (features + w_keyval.shape[1]) // LANES // replicas
    whole = pl.BlockSpec(memory_space=pltpu.VMEM)
    return pl.pallas_call(
        attention_kernel,
        out_shape=(
            jax.ShapeDtypeStruct((nodes, features), BF16),
            jax.ShapeDtypeStruct((replicas, sent, LANES), BF16),
            jax.ShapeDtypeStruct((nodes, features), F32),
        ),
        in_specs=[whole] * 6,
        out_specs=(whole,) * 3,
        scratch_shapes=[pltpu.VMEM((entries, HEADS * nodes), F32)] * 2,
        compiler_params=pltpu.CompilerParams(vmem_limit_bytes=48 * 1024 * 1024),
        name="attention",
    )(node_rows, grad_out, links, table, w_query, w_keyval)


def shards(node_rows, w_query, w_keyval, need_rows, neighbours, grad_out):
    nodes, features = node_rows.shape
    ny, nz, nc, replicas = (lax.axis_size(a) for a in ("y", "z", "c", "x"))
    inner = nz * nc
    owners = ny * inner

    whole = pl.BlockSpec(memory_space=pltpu.VMEM)
    small = pltpu.CompilerParams(vmem_limit_bytes=SMALL)
    rows = jax.ShapeDtypeStruct((nodes, features), BF16)
    kept = pl.pallas_call(
        keep_kernel,
        out_shape=rows,
        in_specs=[whole],
        out_specs=whole,
        compiler_params=small,
        name="keep",
    )(node_rows)
    need_rows, kept = lax.optimization_barrier((need_rows, kept))
    wanted = need_rows.reshape(owners, replicas).T
    my_rows = lax.dynamic_index_in_dim(wanted, lax.axis_index("x"), 0, keepdims=False)
    my_rows = my_rows[None, :]
    outgoing = pl.pallas_call(
        pick_kernel,
        out_shape=jax.ShapeDtypeStruct((owners, features), BF16),
        in_specs=[whole] * 2,
        out_specs=whole,
        compiler_params=small,
        name="pick",
    )(my_rows, kept)
    incoming = exchange(outgoing.reshape(owners, -1, LANES), ("y", "z", "c")).reshape(owners, features)
    table = lax.all_gather(jnp.concatenate([kept, incoming], 0), "x", axis=0, tiled=True)

    attended, partial, dnode = attention(
        kept, grad_out, neighbours.T, table, w_query, w_keyval, replicas
    )

    summed = jnp.sum(exchange(partial, "x").astype(F32), 0)
    back = summed[2 * nodes : 4 * nodes].astype(BF16).reshape(2, ny, nz, nc, LANES)
    grads = summed[4 * nodes :].astype(BF16).reshape(inner, -1, LANES)
    each = grads.shape[1]
    back = back.transpose(3, 2, 0, 1, 4).reshape(inner, 2 * ny, LANES)
    landed = exchange(jnp.concatenate([back, grads], 1), ("c", "z"))
    back = landed[:, : 2 * ny].reshape(inner, 2, ny, LANES).transpose(2, 1, 0, 3)
    back = back.reshape(ny, 2 * inner, LANES)
    grads = jnp.sum(landed[:, 2 * ny :].astype(F32), 0).astype(BF16)
    grads = jnp.broadcast_to(grads[None], (ny, each, LANES))
    landed = exchange(jnp.concatenate([back, grads], 1), "y")
    grads = jnp.sum(landed[:, 2 * inner :].astype(F32), 0).astype(BF16)
    grads = spread(grads, ("x", "z"), nz * replicas)
    grads = grads.reshape(replicas, nz, each, LANES)
    other = lax.ppermute(grads, "c", [(0, 1), (1, 0)])
    core = lax.axis_index("c").reshape(1)
    attended, grad_nodes = pl.pallas_call(
        node_kernel,
        out_shape=(jax.ShapeDtypeStruct((nodes, features), BF16),) * 2,
        in_specs=[whole] * 5,
        out_specs=(whole,) * 2,
        compiler_params=pltpu.CompilerParams(vmem_limit_bytes=SMALL),
        name="node_sums",
    )(my_rows, landed, summed, dnode, attended)
    grad_query, grad_keyval = pl.pallas_call(
        weight_kernel,
        out_shape=(
            jax.ShapeDtypeStruct(w_query.shape, F32),
            jax.ShapeDtypeStruct(w_keyval.shape, F32),
        ),
        in_specs=[pl.BlockSpec(memory_space=pltpu.SMEM)] + [whole] * 2,
        out_specs=(whole,) * 2,
        compiler_params=pltpu.CompilerParams(vmem_limit_bytes=SMALL),
        name="weight_gradients",
    )(core, grads, other)
    return attended, grad_nodes, grad_query, grad_keyval


def solution(mesh):
    own, rep = mesh.devices.shape
    side = math.isqrt(own // 2)
    fine = Mesh(mesh.devices.reshape(side, own // 2 // side, 2, rep), ("y", "z", "c", "x"))
    rows = P(("y", "z", "c", "x"), None)
    in_specs = (rows, P(), P(), P(None, ("y", "z", "c"), None, None), rows, rows)
    return jax.shard_map(
        shards, mesh=fine, in_specs=in_specs, out_specs=(rows, rows, P(), P()), check_vma=False
    )
```

```python
import itertools
import math

import jax
import jax.numpy as jnp
from jax import lax
from jax.experimental import pallas as pl
from jax.experimental.pallas import tpu as pltpu
from jax.sharding import Mesh
from jax.sharding import PartitionSpec as P

HEADS = 4
HEAD_DIM = 64
LANES = 128
CORES = 2
SMALL = 8 * 1024 * 1024
BF16, F32 = jnp.bfloat16, jnp.float32


def dot(a, b, contract=((1,), (0,))):
    return lax.dot_general(a, b, (contract, ((), ())), preferred_element_type=F32)


def rows_of_both(a, b):
    return dot(a, b, ((1,), (1,)))


def columns_of_both(a, b):
    return dot(a, b, ((0,), (0,)))


def exchange(blocks, axes):
    return lax.all_to_all(blocks, axes, split_axis=0, concat_axis=0, tiled=True)


def spread(block, axes, count):
    return exchange(jnp.broadcast_to(block[None], (count,) + block.shape), axes)


def per_head(rows):
    head = lax.broadcasted_iota(jnp.int32, rows.shape, 1) // HEAD_DIM
    wide = rows.astype(F32)
    return jnp.concatenate([jnp.where(head == h, wide, 0.0) for h in range(HEADS)], 0)


def per_pair(values, weights):
    wide, long = weights.shape[1] // (HEADS // 2), 2 * HEAD_DIM
    pairs = [
        columns_of_both(values[:, p * long : (p + 1) * long], weights[:, p * wide : (p + 1) * wide])
        for p in range(HEADS // 2)
    ]
    return jnp.concatenate(pairs, 0)


def own_blocks(table, nodes):
    blocks = [
        table[h * HEAD_DIM : (h + 1) * HEAD_DIM, h % 2 * nodes : (h % 2 + 1) * nodes]
        for h in range(HEADS)
    ]
    return jnp.concatenate(blocks, 0).T


def keep_kernel(node_ref, kept_ref):
    kept_ref[...] = node_ref[...]


def pick_kernel(rows_ref, node_ref, out_ref):
    nodes = node_ref.shape[0]
    picks = lax.broadcasted_iota(jnp.int32, (nodes, rows_ref.shape[1]), 0) == rows_ref[...]
    picks = jnp.where(picks, 1.0, 0.0).astype(BF16)
    out_ref[...] = columns_of_both(picks, node_ref[...]).astype(BF16)


def node_kernel(rows_ref, landed_ref, summed_ref, dnode_ref, attended_in_ref, attended_ref, nodes_ref):
    nodes, features = dnode_ref.shape
    outer, _, lanes = landed_ref.shape
    owners = rows_ref.shape[1]
    inner = owners // outer
    depth = inner // CORES
    attended_ref[...] = attended_in_ref[...]
    picks = lax.broadcasted_iota(jnp.int32, (nodes, owners), 0) == rows_ref[...]
    picks = jnp.where(picks, 1.0, 0.0).astype(BF16)
    given = lax.broadcasted_iota(jnp.int32, (owners, owners), 0)
    asked = lax.broadcasted_iota(jnp.int32, (owners, owners), 1)
    asked = asked // inner * inner + asked % depth * CORES + asked // depth % CORES
    picks = dot(picks, jnp.where(given == asked, 1.0, 0.0).astype(BF16)).astype(BF16)
    for half in range(features // LANES):
        at = slice(half * LANES, (half + 1) * LANES)
        back = landed_ref[:, half * inner : (half + 1) * inner, :].reshape(owners, lanes)
        total = summed_ref[half * nodes : (half + 1) * nodes, :] + dnode_ref[:, at]
        nodes_ref[:, at] = (total + dot(picks, back)).astype(BF16)


def weight_kernel(core_ref, mine_ref, other_ref, grad_q_ref, grad_kv_ref):
    features = grad_q_ref.shape[0]
    replicas, depth, each, _ = mine_ref.shape
    for x, z, c in itertools.product(range(replicas), range(depth), range(CORES)):
        block = jnp.where(core_ref[0] == c, mine_ref[x, z], other_ref[x, z]).astype(F32)
        first = ((x * CORES + c) * depth + z) * each
        for row in range(first, first + each, 8):
            column, at = row // features * LANES, row % features
            to_ref = grad_q_ref if column < features else grad_kv_ref
            column = column if column < features else column - features
            to_ref[at : at + 8, column : column + LANES] = block[row - first : row - first + 8]


def prepare_kernel(node_ref, grad_ref, links_ref, wq_ref, q_ref, g_ref, log_count_ref):
    nodes = node_ref.shape[0]
    degree = links_ref.shape[0]
    replicas = log_count_ref.shape[0] // (2 * nodes)
    block = 2 * nodes
    node = node_ref[...]
    queries = per_head(dot(node, wq_ref[...]).astype(BF16))
    upstream = per_head(grad_ref[...])
    q_ref[...], g_ref[...] = queries.astype(BF16), upstream.astype(BF16)

    links = links_ref[...]
    arrived = links >= replicas * nodes
    owner = jnp.where(arrived, links - replicas * nodes, links) // nodes
    links = owner * block + jnp.where(arrived, nodes, 0) + links % nodes
    for r in range(replicas):
        here = (lax.broadcasted_iota(jnp.int32, (block, nodes), 0) + r * block).astype(jnp.int16)
        count = jnp.zeros((block, nodes), BF16)
        for j in range(degree):
            hit = here == jnp.broadcast_to(links[j : j + 1, :].astype(jnp.int16), here.shape)
            count = count + jnp.where(hit, jnp.ones_like(count), jnp.zeros_like(count))
        count = count.astype(F32)
        log_count = jnp.where(count > 0.0, jnp.log(jnp.maximum(count, 1.0)), -1e30)
        log_count_ref[r * block : (r + 1) * block, :] = log_count


def attention_kernel(
    node_ref, q_ref, g_ref, log_count_ref, table_ref, wq_ref, wkv_ref,
    attended_ref, send_ref, dnode_ref, weight_scr, dprob_scr,
):
    nodes, features = node_ref.shape
    replicas = send_ref.shape[0]
    block = table_ref.shape[0] // replicas
    scale = 1.0 / math.sqrt(HEAD_DIM)
    node = node_ref[...]
    wkv = wkv_ref[...]
    q_heads, g_heads = q_ref[...], g_ref[...]
    q_scaled, g_scaled = (q_heads * scale).astype(BF16), (g_heads * scale).astype(BF16)

    keyval = []
    whole_kv = dot(table_ref[...], wkv).astype(BF16)
    peaks, totals, inners = [], [], []
    for r in range(replicas):
        span = slice(r * block, (r + 1) * block)
        kv = whole_kv[span, :]
        keyval.append(kv)
        log_count = log_count_ref[span, :]
        log_count = jnp.concatenate([log_count] * HEADS, 1)
        score = rows_of_both(kv[:, :features], q_scaled) + log_count
        peaks.append(jnp.max(score, axis=0, keepdims=True))
        weight = jnp.exp(score - peaks[r])
        dprob = rows_of_both(kv[:, features:], g_scaled)
        totals.append(jnp.sum(weight, axis=0, keepdims=True))
        inners.append(jnp.sum(weight * dprob, axis=0, keepdims=True))
        weight_scr[span, :] = weight
        dprob_scr[span, :] = dprob

    peak = peaks[0]
    for other in peaks[1:]:
        peak = jnp.maximum(peak, other)
    factors = [jnp.exp(part - peak) for part in peaks]
    inverse = 1.0 / sum(f * t for f, t in zip(factors, totals))
    factors = [f * inverse for f in factors]
    mean = sum(f * t for f, t in zip(factors, inners))
    attended = jnp.zeros((features, 2 * nodes), F32)
    dquery = jnp.zeros((features, 2 * nodes), F32)
    all_dkv = []
    for r in range(replicas):
        span = slice(r * block, (r + 1) * block)
        kv = keyval[r]
        prob = weight_scr[span, :] * factors[r]
        dscore = (prob * (dprob_scr[span, :] - mean)).astype(BF16)
        prob = prob.astype(BF16)
        attended = attended + per_pair(kv[:, features:], prob)
        dquery = dquery + per_pair(kv[:, :features], dscore)
        dkv = jnp.concatenate([dot(dscore, q_heads), dot(prob, g_heads)], 1).astype(BF16)
        all_dkv.append(dkv)
        dsrc = rows_of_both(dkv, wkv).astype(BF16)
        for part in range(2):
            for half in range(2):
                at = (part * 2 + half) * nodes
                send_ref[r, at : at + nodes, :] = dsrc[
                    part * nodes : (part + 1) * nodes, half * LANES : (half + 1) * LANES
                ]

    grad_kv = columns_of_both(table_ref[...], jnp.concatenate(all_dkv, 0))
    attended_ref[...] = own_blocks(attended, nodes).astype(BF16)
    dquery = own_blocks(dquery, nodes).astype(BF16)
    dnode_ref[...] = rows_of_both(dquery, wq_ref[...])
    grads = jnp.concatenate([columns_of_both(node, dquery), grad_kv], 1).astype(BF16)
    pieces = features * grads.shape[1] // (LANES * LANES)
    each = pieces // replicas
    down = features // LANES
    for piece in range(pieces):
        column, row = (piece // down) * LANES, (piece % down) * LANES
        at = 4 * nodes + (piece % each) * LANES
        send_ref[piece // each, at : at + LANES, :] = grads[row : row + LANES, column : column + LANES]


def prepare(node_rows, grad_out, links, w_query, replicas):
    nodes, features = node_rows.shape
    whole = pl.BlockSpec(memory_space=pltpu.VMEM)
    return pl.pallas_call(
        prepare_kernel,
        out_shape=(jax.ShapeDtypeStruct((HEADS * nodes, features), BF16),) * 2
        + (jax.ShapeDtypeStruct((2 * nodes * replicas, nodes), F32),),
        in_specs=[whole] * 4,
        out_specs=(whole,) * 3,
        compiler_params=pltpu.CompilerParams(vmem_limit_bytes=SMALL),
        cost_estimate=pl.CostEstimate(flops=20000000, bytes_accessed=2000000, transcendentals=130000),
        name="prepare",
    )(node_rows, grad_out, links, w_query)


def attention(node_rows, q_heads, g_heads, log_count, table, w_query, w_keyval, replicas):
    nodes, features = node_rows.shape
    entries = table.shape[0]
    sent = 4 * nodes + features * (features + w_keyval.shape[1]) // LANES // replicas
    whole = pl.BlockSpec(memory_space=pltpu.VMEM)
    return pl.pallas_call(
        attention_kernel,
        out_shape=(
            jax.ShapeDtypeStruct((nodes, features), BF16),
            jax.ShapeDtypeStruct((replicas, sent, LANES), BF16),
            jax.ShapeDtypeStruct((nodes, features), F32),
        ),
        in_specs=[whole] * 7,
        out_specs=(whole,) * 3,
        scratch_shapes=[pltpu.VMEM((entries, HEADS * nodes), F32)] * 2,
        compiler_params=pltpu.CompilerParams(vmem_limit_bytes=48 * 1024 * 1024),
        name="attention",
    )(node_rows, q_heads, g_heads, log_count, table, w_query, w_keyval)


def shards(node_rows, w_query, w_keyval, need_rows, neighbours, grad_out):
    nodes, features = node_rows.shape
    ny, nz, nc, replicas = (lax.axis_size(a) for a in ("y", "z", "c", "x"))
    inner = nz * nc
    owners = ny * inner

    whole = pl.BlockSpec(memory_space=pltpu.VMEM)
    small = pltpu.CompilerParams(vmem_limit_bytes=SMALL)
    rows = jax.ShapeDtypeStruct((nodes, features), BF16)
    kept = pl.pallas_call(
        keep_kernel,
        out_shape=rows,
        in_specs=[whole],
        out_specs=whole,
        compiler_params=small,
        name="keep",
    )(node_rows)
    need_rows, kept = lax.optimization_barrier((need_rows, kept))
    wanted = need_rows.reshape(owners, replicas).T
    my_rows = lax.dynamic_index_in_dim(wanted, lax.axis_index("x"), 0, keepdims=False)
    my_rows = my_rows[None, :]
    outgoing = pl.pallas_call(
        pick_kernel,
        out_shape=jax.ShapeDtypeStruct((owners, features), BF16),
        in_specs=[whole] * 2,
        out_specs=whole,
        compiler_params=small,
        name="pick",
    )(my_rows, kept)
    incoming = exchange(outgoing.reshape(owners, -1, LANES), ("y", "z", "c")).reshape(owners, features)
    table = lax.all_gather(jnp.concatenate([kept, incoming], 0), "x", axis=0, tiled=True)

    ready = prepare(kept, grad_out, neighbours.T, w_query, replicas)
    attended, partial, dnode = attention(kept, *ready, table, w_query, w_keyval, replicas)

    summed = jnp.sum(exchange(partial, "x").astype(F32), 0)
    back = summed[2 * nodes : 4 * nodes].astype(BF16).reshape(2, ny, nz, nc, LANES)
    grads = summed[4 * nodes :].astype(BF16).reshape(inner, -1, LANES)
    each = grads.shape[1]
    back = back.transpose(3, 2, 0, 1, 4).reshape(inner, 2 * ny, LANES)
    landed = exchange(jnp.concatenate([back, grads], 1), ("c", "z"))
    back = landed[:, : 2 * ny].reshape(inner, 2, ny, LANES).transpose(2, 1, 0, 3)
    back = back.reshape(ny, 2 * inner, LANES)
    grads = jnp.sum(landed[:, 2 * ny :].astype(F32), 0).astype(BF16)
    grads = jnp.broadcast_to(grads[None], (ny, each, LANES))
    landed = exchange(jnp.concatenate([back, grads], 1), "y")
    grads = jnp.sum(landed[:, 2 * inner :].astype(F32), 0).astype(BF16)
    grads = spread(grads, ("x", "z"), nz * replicas)
    grads = grads.reshape(replicas, nz, each, LANES)
    other = lax.ppermute(grads, "c", [(0, 1), (1, 0)])
    core = lax.axis_index("c").reshape(1)
    attended, grad_nodes = pl.pallas_call(
        node_kernel,
        out_shape=(jax.ShapeDtypeStruct((nodes, features), BF16),) * 2,
        in_specs=[whole] * 5,
        out_specs=(whole,) * 2,
        compiler_params=pltpu.CompilerParams(vmem_limit_bytes=SMALL),
        name="node_sums",
    )(my_rows, landed, summed, dnode, attended)
    grad_query, grad_keyval = pl.pallas_call(
        weight_kernel,
        out_shape=(
            jax.ShapeDtypeStruct(w_query.shape, F32),
            jax.ShapeDtypeStruct(w_keyval.shape, F32),
        ),
        in_specs=[pl.BlockSpec(memory_space=pltpu.SMEM)] + [whole] * 2,
        out_specs=(whole,) * 2,
        compiler_params=pltpu.CompilerParams(vmem_limit_bytes=SMALL),
        name="weight_gradients",
    )(core, grads, other)
    return attended, grad_nodes, grad_query, grad_keyval


def solution(mesh):
    own, rep = mesh.devices.shape
    side = math.isqrt(own // 2)
    fine = Mesh(mesh.devices.reshape(side, own // 2 // side, 2, rep), ("y", "z", "c", "x"))
    rows = P(("y", "z", "c", "x"), None)
    in_specs = (rows, P(), P(), P(None, ("y", "z", "c"), None, None), rows, rows)
    return jax.shard_map(
        shards, mesh=fine, in_specs=in_specs, out_specs=(rows, rows, P(), P()), check_vma=False
    )
```

```python
import itertools
import math

import jax
import jax.numpy as jnp
from jax import lax
from jax.experimental import pallas as pl
from jax.experimental.pallas import tpu as pltpu
from jax.sharding import Mesh
from jax.sharding import PartitionSpec as P

HEADS = 4
HEAD_DIM = 64
LANES = 128
CORES = 2
SMALL = 8 * 1024 * 1024
BF16, F32 = jnp.bfloat16, jnp.float32


def dot(a, b, contract=((1,), (0,))):
    return lax.dot_general(a, b, (contract, ((), ())), preferred_element_type=F32)


def rows_of_both(a, b):
    return dot(a, b, ((1,), (1,)))


def columns_of_both(a, b):
    return dot(a, b, ((0,), (0,)))


def exchange(blocks, axes):
    return lax.all_to_all(blocks, axes, split_axis=0, concat_axis=0, tiled=True)


def spread(block, axes, count):
    return exchange(jnp.broadcast_to(block[None], (count,) + block.shape), axes)


def per_head(rows):
    head = lax.broadcasted_iota(jnp.int32, rows.shape, 1) // HEAD_DIM
    wide = rows.astype(F32)
    return jnp.concatenate([jnp.where(head == h, wide, 0.0) for h in range(HEADS)], 0)


def per_pair(values, weights):
    wide, long = weights.shape[1] // (HEADS // 2), 2 * HEAD_DIM
    pairs = [
        columns_of_both(values[:, p * long : (p + 1) * long], weights[:, p * wide : (p + 1) * wide])
        for p in range(HEADS // 2)
    ]
    return jnp.concatenate(pairs, 0)


def own_blocks(table, nodes):
    blocks = [
        table[h * HEAD_DIM : (h + 1) * HEAD_DIM, h % 2 * nodes : (h % 2 + 1) * nodes]
        for h in range(HEADS)
    ]
    return jnp.concatenate(blocks, 0).T


def keep_kernel(node_ref, kept_ref):
    kept_ref[...] = node_ref[...]


def pick_kernel(rows_ref, node_ref, out_ref):
    nodes = node_ref.shape[0]
    picks = lax.broadcasted_iota(jnp.int32, (nodes, rows_ref.shape[1]), 0) == rows_ref[...]
    picks = jnp.where(picks, 1.0, 0.0).astype(BF16)
    out_ref[...] = columns_of_both(picks, node_ref[...]).astype(BF16)


def node_kernel(rows_ref, landed_ref, summed_ref, dnode_ref, attended_in_ref, attended_ref, nodes_ref):
    nodes, features = dnode_ref.shape
    outer, _, lanes = landed_ref.shape
    owners = rows_ref.shape[1]
    inner = owners // outer
    depth = inner // CORES
    attended_ref[...] = attended_in_ref[...]
    picks = lax.broadcasted_iota(jnp.int32, (nodes, owners), 0) == rows_ref[...]
    picks = jnp.where(picks, 1.0, 0.0).astype(BF16)
    given = lax.broadcasted_iota(jnp.int32, (owners, owners), 0)
    asked = lax.broadcasted_iota(jnp.int32, (owners, owners), 1)
    asked = asked // inner * inner + asked % depth * CORES + asked // depth % CORES
    picks = dot(picks, jnp.where(given == asked, 1.0, 0.0).astype(BF16)).astype(BF16)
    for half in range(features // LANES):
        at = slice(half * LANES, (half + 1) * LANES)
        back = landed_ref[:, half * inner : (half + 1) * inner, :].reshape(owners, lanes)
        total = summed_ref[half * nodes : (half + 1) * nodes, :] + dnode_ref[:, at]
        nodes_ref[:, at] = (total + dot(picks, back)).astype(BF16)


def weight_kernel(core_ref, mine_ref, other_ref, grad_q_ref, grad_kv_ref):
    features = grad_q_ref.shape[0]
    replicas, depth, each, _ = mine_ref.shape
    for x, z, c in itertools.product(range(replicas), range(depth), range(CORES)):
        block = jnp.where(core_ref[0] == c, mine_ref[x, z], other_ref[x, z]).astype(F32)
        first = ((x * CORES + c) * depth + z) * each
        for row in range(first, first + each, 8):
            column, at = row // features * LANES, row % features
            to_ref = grad_q_ref if column < features else grad_kv_ref
            column = column if column < features else column - features
            to_ref[at : at + 8, column : column + LANES] = block[row - first : row - first + 8]


def attention_kernel(
    node_ref, grad_ref, links_ref, table_ref, wq_ref, wkv_ref,
    attended_ref, send_ref, dnode_ref, weight_scr, dprob_scr,
):
    nodes, features = node_ref.shape
    degree = links_ref.shape[0]
    replicas = send_ref.shape[0]
    block = table_ref.shape[0] // replicas
    scale = 1.0 / math.sqrt(HEAD_DIM)
    node = node_ref[...]
    wkv = wkv_ref[...]
    queries = per_head(dot(node, wq_ref[...]).astype(BF16))
    upstream = per_head(grad_ref[...])
    q_heads, q_scaled = queries.astype(BF16), (queries * scale).astype(BF16)
    g_heads, g_scaled = upstream.astype(BF16), (upstream * scale).astype(BF16)

    links = links_ref[...]
    arrived = links >= replicas * nodes
    owner = jnp.where(arrived, links - replicas * nodes, links) // nodes
    links = owner * block + jnp.where(arrived, nodes, 0) + links % nodes

    keyval = []
    whole_kv = dot(table_ref[...], wkv).astype(BF16)
    peaks, totals, inners = [], [], []
    for r in range(replicas):
        span = slice(r * block, (r + 1) * block)
        kv = whole_kv[span, :]
        keyval.append(kv)
        here = (lax.broadcasted_iota(jnp.int32, (block, nodes), 0) + r * block).astype(jnp.int16)
        count = jnp.zeros((block, nodes), BF16)
        for j in range(degree):
            hit = here == jnp.broadcast_to(links[j : j + 1, :].astype(jnp.int16), here.shape)
            count = count + jnp.where(hit, jnp.ones_like(count), jnp.zeros_like(count))
        count = count.astype(F32)
        log_count = jnp.maximum(jnp.log(count), -1e30)
        log_count = jnp.concatenate([log_count] * HEADS, 1)
        score = rows_of_both(kv[:, :features], q_scaled) + log_count
        peaks.append(jnp.max(score, axis=0, keepdims=True))
        weight = jnp.exp(score - peaks[r])
        dprob = rows_of_both(kv[:, features:], g_scaled)
        totals.append(jnp.sum(weight, axis=0, keepdims=True))
        inners.append(jnp.sum(weight * dprob, axis=0, keepdims=True))
        weight_scr[span, :] = weight
        dprob_scr[span, :] = dprob

    peak = peaks[0]
    for other in peaks[1:]:
        peak = jnp.maximum(peak, other)
    factors = [jnp.exp(part - peak) for part in peaks]
    inverse = 1.0 / sum(f * t for f, t in zip(factors, totals))
    factors = [f * inverse for f in factors]
    mean = sum(f * t for f, t in zip(factors, inners))
    attended = jnp.zeros((features, 2 * nodes), F32)
    dquery = jnp.zeros((features, 2 * nodes), F32)
    all_dkv = []
    for r in range(replicas):
        span = slice(r * block, (r + 1) * block)
        kv = keyval[r]
        prob = weight_scr[span, :] * factors[r]
        dscore = (prob * (dprob_scr[span, :] - mean)).astype(BF16)
        prob = prob.astype(BF16)
        attended = attended + per_pair(kv[:, features:], prob)
        dquery = dquery + per_pair(kv[:, :features], dscore)
        dkv = jnp.concatenate([dot(dscore, q_heads), dot(prob, g_heads)], 1).astype(BF16)
        all_dkv.append(dkv)
        dsrc = rows_of_both(dkv, wkv).astype(BF16)
        for part in range(2):
            for half in range(2):
                at = (part * 2 + half) * nodes
                send_ref[r, at : at + nodes, :] = dsrc[
                    part * nodes : (part + 1) * nodes, half * LANES : (half + 1) * LANES
                ]

    grad_kv = columns_of_both(table_ref[...], jnp.concatenate(all_dkv, 0))
    attended_ref[...] = own_blocks(attended, nodes).astype(BF16)
    dquery = own_blocks(dquery, nodes).astype(BF16)
    dnode_ref[...] = rows_of_both(dquery, wq_ref[...])
    grads = jnp.concatenate([columns_of_both(node, dquery), grad_kv], 1).astype(BF16)
    pieces = features * grads.shape[1] // (LANES * LANES)
    each = pieces // replicas
    down = features // LANES
    for piece in range(pieces):
        column, row = (piece // down) * LANES, (piece % down) * LANES
        at = 4 * nodes + (piece % each) * LANES
        send_ref[piece // each, at : at + LANES, :] = grads[row : row + LANES, column : column + LANES]


def attention(node_rows, grad_out, links, table, w_query, w_keyval, replicas):
    nodes, features = node_rows.shape
    entries = table.shape[0]
    sent = 4 * nodes + features * (features + w_keyval.shape[1]) // LANES // replicas
    whole = pl.BlockSpec(memory_space=pltpu.VMEM)
    return pl.pallas_call(
        attention_kernel,
        out_shape=(
            jax.ShapeDtypeStruct((nodes, features), BF16),
            jax.ShapeDtypeStruct((replicas, sent, LANES), BF16),
            jax.ShapeDtypeStruct((nodes, features), F32),
        ),
        in_specs=[whole] * 6,
        out_specs=(whole,) * 3,
        scratch_shapes=[pltpu.VMEM((entries, HEADS * nodes), F32)] * 2,
        compiler_params=pltpu.CompilerParams(vmem_limit_bytes=48 * 1024 * 1024),
        name="attention",
    )(node_rows, grad_out, links, table, w_query, w_keyval)


def shards(node_rows, w_query, w_keyval, need_rows, neighbours, grad_out):
    nodes, features = node_rows.shape
    ny, nz, nc, replicas = (lax.axis_size(a) for a in ("y", "z", "c", "x"))
    inner = nz * nc
    owners = ny * inner

    whole = pl.BlockSpec(memory_space=pltpu.VMEM)
    small = pltpu.CompilerParams(vmem_limit_bytes=SMALL)
    rows = jax.ShapeDtypeStruct((nodes, features), BF16)
    kept = pl.pallas_call(
        keep_kernel,
        out_shape=rows,
        in_specs=[whole],
        out_specs=whole,
        compiler_params=small,
        name="keep",
    )(node_rows)
    need_rows, kept = lax.optimization_barrier((need_rows, kept))
    wanted = need_rows.reshape(owners, replicas).T
    my_rows = lax.dynamic_index_in_dim(wanted, lax.axis_index("x"), 0, keepdims=False)
    my_rows = my_rows[None, :]
    outgoing = pl.pallas_call(
        pick_kernel,
        out_shape=jax.ShapeDtypeStruct((owners, features), BF16),
        in_specs=[whole] * 2,
        out_specs=whole,
        compiler_params=small,
        name="pick",
    )(my_rows, kept)
    incoming = exchange(outgoing.reshape(owners, -1, LANES), ("y", "z", "c")).reshape(owners, features)
    table = lax.all_gather(jnp.concatenate([kept, incoming], 0), "x", axis=0, tiled=True)

    attended, partial, dnode = attention(
        kept, grad_out, neighbours.T, table, w_query, w_keyval, replicas
    )

    summed = jnp.sum(exchange(partial, "x").astype(F32), 0)
    back = summed[2 * nodes : 4 * nodes].astype(BF16).reshape(2, ny, nz, nc, LANES)
    grads = summed[4 * nodes :].astype(BF16).reshape(inner, -1, LANES)
    each = grads.shape[1]
    back = back.transpose(3, 2, 0, 1, 4).reshape(inner, 2 * ny, LANES)
    landed = exchange(jnp.concatenate([back, grads], 1), ("c", "z"))
    back = landed[:, : 2 * ny].reshape(inner, 2, ny, LANES).transpose(2, 1, 0, 3)
    back = back.reshape(ny, 2 * inner, LANES)
    grads = jnp.sum(landed[:, 2 * ny :].astype(F32), 0).astype(BF16)
    grads = jnp.broadcast_to(grads[None], (ny, each, LANES))
    landed = exchange(jnp.concatenate([back, grads], 1), "y")
    grads = jnp.sum(landed[:, 2 * inner :].astype(F32), 0).astype(BF16)
    grads = spread(grads, ("x", "z"), nz * replicas)
    grads = grads.reshape(replicas, nz, each, LANES)
    other = lax.ppermute(grads, "c", [(0, 1), (1, 0)])
    core = lax.axis_index("c").reshape(1)
    attended, grad_nodes = pl.pallas_call(
        node_kernel,
        out_shape=(jax.ShapeDtypeStruct((nodes, features), BF16),) * 2,
        in_specs=[whole] * 5,
        out_specs=(whole,) * 2,
        compiler_params=pltpu.CompilerParams(vmem_limit_bytes=SMALL),
        name="node_sums",
    )(my_rows, landed, summed, dnode, attended)
    grad_query, grad_keyval = pl.pallas_call(
        weight_kernel,
        out_shape=(
            jax.ShapeDtypeStruct(w_query.shape, F32),
            jax.ShapeDtypeStruct(w_keyval.shape, F32),
        ),
        in_specs=[pl.BlockSpec(memory_space=pltpu.SMEM)] + [whole] * 2,
        out_specs=(whole,) * 2,
        compiler_params=pltpu.CompilerParams(vmem_limit_bytes=SMALL),
        name="weight_gradients",
    )(core, grads, other)
    return attended, grad_nodes, grad_query, grad_keyval


def solution(mesh):
    own, rep = mesh.devices.shape
    side = math.isqrt(own // 2)
    fine = Mesh(mesh.devices.reshape(side, own // 2 // side, 2, rep), ("y", "z", "c", "x"))
    rows = P(("y", "z", "c", "x"), None)
    in_specs = (rows, P(), P(), P(None, ("y", "z", "c"), None, None), rows, rows)
    return jax.shard_map(
        shards, mesh=fine, in_specs=in_specs, out_specs=(rows, rows, P(), P()), check_vma=False
    )
```
